512 devices in a mesh: row: 32 (over y_lo, z), col: 16 (over x, y_hi, core).
Axes of the slice: x: 4, y: 8 (y_hi: 2, y_lo: 4; y = y_hi * 4 + y_lo), z: 8, core: 2. Of those that a mesh axis runs over, the one named last changes fastest.
Arguments:
- mask_field: float32 [8192, 2048], P('row', 'col'), may hold values from 0 to 1
- target: int32 [8192, 2048], P('row', 'col'), may hold values 0 or 1
- kernel_real: float32 [4, 128, 128], replicated, may hold values from -0.046875 to 0.046875
- kernel_imag: float32 [4, 128, 128], replicated, may hold values from -0.046875 to 0.046875
Outputs:
- aerial: float32 [8192, 2048], P('row', 'col')
- gradient: float32 [8192, 2048], P('row', 'col')
The draws below stay inside these ranges and needn't reach their ends.
All inputs are finite; a program needn't handle non-finite values. No bound on the sum of `target` on one device may be relied on, other than what follows from the above.
Results may differ from the reference program's by a relative error of at most 0.00012.
Values sent between devices are 32-bit elements; how exact they have to be, the bound alone decides.
A program may use at most 64 MiB of HBM per device.

```python
import jax
import jax.numpy as jnp
from jax import lax

KERNELS = 4
SUPPORT = 128
NX = 8192
NY = 2048


def place_ends(result, key, low, top_value):
    longest = result.shape.index(max(result.shape))
    spots = []
    for shift in (0, 1):
        where = [jax.random.randint(jax.random.fold_in(key, axis), (), 0, length) for axis, length in enumerate(result.shape)]
        where[longest] = (where[longest] + shift) % result.shape[longest]
        spots.append(tuple(where))
    return result.at[spots[0]].set(low).at[spots[1]].set(top_value)


def block_scale(stream_key, dims, pieces, least, top_value):
    def one(dim, blocks):
        heights = jax.random.uniform(jax.random.fold_in(jax.random.fold_in(stream_key, 6), dim), (blocks,), jnp.float32, least / len(pieces), top_value / len(pieces))
        return jnp.repeat(jnp.exp(heights), dims[dim] // blocks).reshape((-1,) + (1,) * (len(dims) - dim - 1))

    loudness = one(*pieces[0])
    for cut in pieces[1:]:
        loudness = loudness * one(*cut)
    return loudness


def bell_draw(own_key, dims, scale, bound, kind=jnp.bfloat16):
    entries = jax.random.normal(own_key, dims, jnp.float32) * scale
    return jnp.minimum(jnp.maximum(entries, -bound), bound).astype(kind)


def setup_inputs(seed: int = 0) -> dict:
    streams_of = jax.random.split(jax.random.key(seed), 5)
    mask_field = jnp.clip(1.0 * jax.random.uniform(streams_of[0], (NX, NY), jnp.float32) ** block_scale(streams_of[0], (NX, NY), ((0, 32), (1, 16)), -0.2, 0.2), 0.0, 1.0)
    target = place_ends((jax.random.randint(streams_of[1], (NX, NY), 0, 2) < 1).astype(jnp.int32), jax.random.fold_in(streams_of[1], 1), 0, 1)
    kernel_real = bell_draw(streams_of[2], (KERNELS, SUPPORT, SUPPORT), (SUPPORT * SUPPORT) ** -0.5, 0.046875, jnp.float32)
    kernel_imag = bell_draw(streams_of[3], (KERNELS, SUPPORT, SUPPORT), (SUPPORT * SUPPORT) ** -0.5, 0.046875, jnp.float32)
    return dict(mask_field=mask_field, target=target, kernel_real=kernel_real, kernel_imag=kernel_imag)


def reference(mask_field, target, kernel_real, kernel_imag):
    grid_rows, grid_cols = mask_field.shape
    kernel_count, support, _ = kernel_real.shape
    margin = support // 2
    full_rows = grid_rows + support
    full_cols = grid_cols + support
    padded = jnp.zeros((full_rows, full_cols), jnp.float32)
    padded = padded.at[margin:margin + grid_rows, margin:margin + grid_cols].set(mask_field)
    mask_spectrum = jnp.fft.fft2(padded)
    amplitudes = []
    kernel_spectra = []
    aerial = jnp.zeros((grid_rows, grid_cols), jnp.float32)
    for number in range(kernel_count):
        kernel = lax.complex(kernel_real[number], kernel_imag[number])
        kernel_padded = jnp.zeros((full_rows, full_cols), kernel.dtype).at[:support, :support].set(kernel)
        plus_spectrum = jnp.conj(jnp.fft.fft2(jnp.conj(kernel_padded)))
        kernel_spectra.append(jnp.fft.fft2(kernel_padded))
        amplitude = jnp.fft.ifft2(mask_spectrum * plus_spectrum)[:grid_rows, :grid_cols]
        amplitudes.append(amplitude)
        aerial = aerial + (jnp.real(amplitude) ** 2 + jnp.imag(amplitude) ** 2).astype(jnp.float32)
    resist = jax.nn.sigmoid(1.5 * (aerial - 2.7))
    slope_field = 2.0 * (resist - target.astype(jnp.float32)) * 1.5 * resist * (1.0 - resist)
    total_spectrum = jnp.zeros((full_rows, full_cols), mask_spectrum.dtype)
    for number in range(kernel_count):
        weighted = slope_field * jnp.conj(amplitudes[number])
        weighted_padded = jnp.zeros((full_rows, full_cols), weighted.dtype).at[:grid_rows, :grid_cols].set(weighted)
        total_spectrum = total_spectrum + jnp.fft.fft2(weighted_padded) * kernel_spectra[number]
    convolved = jnp.fft.ifft2(total_spectrum)[margin:margin + grid_rows, margin:margin + grid_cols]
    gradient = (2.0 * jnp.real(convolved)).astype(jnp.float32)
    return aerial, gradient
```

```python
import jax
import jax.numpy as jnp
import ml_dtypes
import numpy as np
from jax import lax
from jax.experimental import pallas as pl
from jax.experimental.pallas import tpu as pltpu
from jax.sharding import PartitionSpec as P

F32, BF16 = jnp.float32, jnp.bfloat16
MESH = pl.DeviceIdType.MESH
steepness = 1.5
threshold = 2.7


def split_table(table):
    high = table.astype(ml_dtypes.bfloat16)
    return high, (table - high.astype(np.float64)).astype(ml_dtypes.bfloat16)


def tables():
    freq = 2 * np.pi * (np.arange(128) + 0.5) / 256
    col = np.arange(256)
    col = np.where(col < 192, col, col - 256)
    tap = np.arange(128) - 64
    row = np.arange(256)
    cat = np.concatenate
    wm_h, wm_l = split_table(cat([np.cos(np.outer(col, freq)), np.sin(np.outer(col, freq))], 1))
    wk_h, wk_l = split_table(cat([np.cos(np.outer(tap, freq)), np.sin(np.outer(tap, freq))], 1))
    cs = cat([np.cos(np.outer(freq, row)), np.sin(np.outer(freq, row))], 0)
    cs_h, cs_l = split_table(cs)
    l2_h, l2_l = split_table(cs.T)
    wi_h, wi_l = split_table(cat([np.cos(np.outer(freq, col)), -np.sin(np.outer(freq, col))], 0) / 32768.0)
    return dict(
        wk_hh=cat([wk_h, wk_h], 0),
        wk_l=wk_l,
        ca_hh=cat([cs_h[:, :128], cs_h[:, :128]], 1),
        cs_l=cs_l,
        wm_h=wm_h,
        wm_l=wm_l,
        cs_h=cs_h,
        l2_h=l2_h,
        l2_l=l2_l,
        wiy_hl=cat([wi_h[:, :128], wi_l[:, :128]], 1),
        wi_h=wi_h,
        wi_l=wi_l,
        wy_hh=cat([wm_h[:128], wm_h[:128]], 0),
    )


TABLES = tables()
GROUPS = (("wk_hh", "wk_l", "ca_hh", "cs_l"), ("wm_h", "wm_l", "cs_h", "l2_h", "l2_l", "wiy_hl", "wi_h", "wi_l", "wy_hh"))
PACKED = [np.concatenate([TABLES[name] for name in group], 0) for group in GROUPS]


def views(refs):
    out = {}
    for group, ref in zip(GROUPS, refs):
        start = 0
        for name in group:
            size = TABLES[name].shape[0]
            out[name] = ref.at[start : start + size]
            start += size
    out["ca_l"] = out["cs_l"].at[:, :128]
    out["wy_l"] = out["wm_l"].at[:128]
    out["wiy_h"] = out["wi_h"].at[:, :128]
    return out


def dot(a, b):
    return jnp.dot(a, b, preferred_element_type=F32)

def split(x):
    hi = x.astype(BF16)
    lo = (x - hi.astype(F32)).astype(BF16)
    return hi, lo

def lanes(a, b):
    return jnp.concatenate([a, b], axis=1)

def rows(a, b):
    return jnp.concatenate([a, b], axis=0)

def butterfly(o):
    P, Q, R, T = o[:128, :128], o[:128, 128:], o[128:, :128], o[128:, 128:]
    return P - T, Q + R, P + T, Q - R

def do_kernel_columns(t, k_ref, c_s):
    for part in range(2):
        for k in range(4):
            xh, xl = split(k_ref[part, k])
            c = dot(lanes(xh, xl), t['wk_hh'][...]) + dot(xh, t['wk_l'][...])
            c_s[2*k+part, :128], c_s[2*k+part, 128:] = split(c)

def do_kernel_rows(t, H, c_s):
    for j in range(8):
        o = dot(t['ca_hh'][...], c_s[j]) + dot(t['ca_l'][...], c_s[j, :128])
        for n, v in enumerate(butterfly(o)):
            H[j, n] = v

def do_mask(t, E, M):
    xh, xl = split(lanes(E[0], E[1]))
    c = dot(xh, t['wm_h'][...]) + dot(xl, t['wm_h'][...]) + dot(xh, t['wm_l'][...])
    for r in range(2):
        ch, cl = split(c[128*r:128*r+256])
        o = dot(t['cs_h'][...], ch) + dot(t['cs_h'][...], cl) + dot(t['cs_l'][...], ch)
        for n, v in enumerate(butterfly(o)):
            M[r, n] = v

def do_fields(t, H, M, f, r, d_s, z_s):
    for j in range(8):
        def prod(n):
            mr, mi, hr, hi = M[r, n], M[r, n+1], H[j, n], H[j, n+1]
            return mr*hr + mi*hi, mr*hi - mi*hr
        fr_p, fi_p = prod(0)
        fr_m, fi_m = prod(2)
        d = rows(lanes(fr_p+fr_m, fi_p+fi_m), lanes(fi_m-fi_p, fr_p-fr_m))
        d_s[0, j], d_s[1, j] = split(d)
        dh, dl = d_s[0, j], d_s[1, j]
        z = dot(t['l2_h'][:128], dh) + dot(t['l2_h'][:128], dl) + dot(t['l2_l'][:128], dh)
        z_s[0, j], z_s[1, j] = split(z)
    for j in range(8):
        a = dot(z_s[0, j], t['wiy_hl'][...])
        f[r, j] = a[:, :128] + a[:, 128:] + dot(z_s[1, j], t['wiy_h'][...])

def do_slope(f, target, aerial, slope, r):
    a = f[r, 0]*f[r, 0]
    for j in range(1, 8):
        a = a + f[r, j]*f[r, j]
    aerial[128*r:128*r+128] = a
    res = jax.nn.sigmoid(steepness*(a-threshold))
    slope[r] = 2.0*(res-target[128*r:128*r+128].astype(F32))*steepness*res*(1.0-res)

def do_back(t, H, f, slope, T, r, c_s):
    for j in range(8):
        g = slope[r]*f[r, j]
        gh, gl = split(g)
        c = dot(lanes(gh, gl), t['wy_hh'][...]) + dot(gh, t['wy_l'][...])
        c_s[j, :128], c_s[j, 128:] = split(c)
    for j in range(8):
        o = dot(t['ca_hh'][...], c_s[j]) + dot(t['ca_l'][...], c_s[j, :128])
        b = butterfly(o)
        for n in (0, 2):
            gr, gi, hr, hi = b[n], b[n+1], H[j, n], H[j, n+1]
            tr, ti = gr*hr - gi*hi, gr*hi + gi*hr
            if j:
                tr, ti = tr + T[r, n], ti + T[r, n+1]
            T[r, n], T[r, n+1] = tr, ti

def do_final(t, T, r):
    rp, ip, rm, im = T[r, 0], T[r, 1], T[r, 2], T[r, 3]
    d = 2.0*rows(lanes(rp+rm, -(ip+im)), lanes(ip-im, rp-rm))
    dh, dl = split(d)
    z = dot(t['l2_h'][...], dh) + dot(t['l2_h'][...], dl) + dot(t['l2_l'][...], dh)
    zh, zl = split(z)
    return dot(zh, t['wi_h'][...]) + dot(zl, t['wi_h'][...]) + dot(zh, t['wi_l'][...])

def swap(x):
    return pltpu.roll(x, 64, 1)

def kernel(mask, target, kr, ki, tab_a, tab_b, aerial, gradient,
           E, target_v, k_v, ta_v, tb_v, H, M, f, slope, T, c_s, d_s, z_s, C,
           aerial_v, grad_v, side, PS, PV, FU, FD, GS, GV, local_sem, send_sem, recv_sem):
    r, c = lax.axis_index("row"), lax.axis_index("col")
    nr, nc = lax.axis_size("row"), lax.axis_size("col")
    up, down, left, right = r > 0, r < nr - 1, c > 0, c < nc - 1
    up_id, down_id, left_id, right_id = (r - 1, c), (r + 1, c), (r, c - 1), (r, c + 1)
    everyone = ((up, up_id), (down, down_id), (left, left_id), (right, right_id))

    local = []
    for n, (src, dst) in enumerate(((mask, E.at[0, pl.ds(64, 256)]), (kr, k_v.at[0]), (ki, k_v.at[1]),
                                    (tab_a, ta_v), (tab_b, tb_v), (target, target_v))):
        local.append(pltpu.make_async_copy(src, dst, local_sem.at[n]))
        local[-1].start()

    barrier = pltpu.get_barrier_semaphore()
    for there, device in everyone:
        @pl.when(there)
        def _():
            pl.semaphore_signal(barrier, inc=1, device_id=device, device_id_type=MESH)

    def edge(cond, ref):
        @pl.when(jnp.logical_not(cond))
        def _():
            ref[...] = jnp.zeros(ref.shape, F32)

    edge(right, PV.at[0]); edge(left, PV.at[1]); edge(right, GV.at[0]); edge(left, GV.at[1])
    edge(up, FU); edge(down, FD)
    edge(up, E.at[:, pl.ds(0, 64)]); edge(down, E.at[:, pl.ds(320, 64)])

    def remote(n, src, dst, device):
        return pltpu.make_async_remote_copy(src_ref=src, dst_ref=dst, send_sem=send_sem.at[n],
                                            recv_sem=recv_sem.at[n], device_id=device, device_id_type=MESH)

    def toward(n, which, src, dst):
        go, come, device = {"right": (right, left, right_id), "left": (left, right, left_id),
                            "up": (up, down, up_id), "down": (down, up, down_id)}[which]
        return remote(n, src, dst, device), go, come

    def start(message):
        copy, go, _ = message
        @pl.when(go)
        def _():
            copy.start()

    def wait_recv(message):
        copy, _, come = message
        @pl.when(come)
        def _():
            copy.wait_recv()

    def wait_send(message):
        copy, go, _ = message
        @pl.when(go)
        def _():
            copy.wait_send()

    lane = lax.broadcasted_iota(jnp.int32, (64, 128), 1)
    low = lane < 64

    pairs = ((64, 256), (128, 192))
    local[0].wait()
    for k, (p, q) in enumerate(pairs):
        first, second = E[0, p:p+64], swap(E[0, q:q+64])
        PS[0, k] = jnp.where(low, second, first)
        PS[1, k] = jnp.where(low, first, second)
    pl.semaphore_wait(barrier, sum(there.astype(jnp.int32) for there, _ in everyone))
    cols = [(toward(2*k, "right", PS.at[0, k], PV.at[1, k]), toward(2*k+1, "left", PS.at[1, k], PV.at[0, k]))
            for k in range(2)]
    plain = (toward(4, "up", E.at[0, pl.ds(64, 64)], E.at[0, pl.ds(320, 64)]),
             toward(5, "down", E.at[0, pl.ds(256, 64)], E.at[0, pl.ds(0, 64)]))
    corner = (toward(6, "up", E.at[1, pl.ds(64, 64)], E.at[1, pl.ds(320, 64)]),
              toward(7, "down", E.at[1, pl.ds(256, 64)], E.at[1, pl.ds(0, 64)]))
    for message in (*cols[0], *plain, *cols[1]):
        start(message)

    t = views((ta_v, tb_v))
    for n in (1, 2, 3):
        local[n].wait()
    do_kernel_columns(t, k_v, c_s.at[0])

    def unpack(k):
        p, q = pairs[k]
        for message in cols[k]:
            wait_recv(message)
        E[1, p:p+64] = jnp.where(low, PV[0, k], PV[1, k])
        E[1, q:q+64] = swap(jnp.where(low, PV[1, k], PV[0, k]))

    unpack(0)
    for message in corner:
        start(message)
    do_kernel_rows(t, H, c_s.at[0])
    unpack(1)
    for message in (*plain, *corner):
        wait_recv(message)
    local[4].wait()
    do_mask(t, E, M)
    local[5].wait()

    gradient_up = toward(8, "up", C.at[0, pl.ds(0, 64)], FD)
    gradient_down = toward(9, "down", C.at[1, pl.ds(192, 64)], FU)
    for b in range(2):
        do_fields(t, H, M, f, b, d_s.at[b], z_s.at[b])
        do_slope(f, target_v, aerial_v, slope, b)
        do_back(t, H, f, slope, T, b, c_s.at[1+b])
        C[b] = do_final(t, T, b)
        start(gradient_up if b == 0 else gradient_down)
    aerial_out = pltpu.make_async_copy(aerial_v, aerial, local_sem.at[6])
    aerial_out.start()

    def place(p, total):
        grad_v[p:p+64] = total[:, :128]
        side[p:p+64] = total[:, 128:]

    def send_sides(k, p, q):
        first, second = side[p:p+64], swap(side[q:q+64])
        GS[0, k] = jnp.where(low, first, second)
        GS[1, k] = jnp.where(low, second, first)
        messages = (toward(10+2*k, "right", GS.at[0, k], GV.at[1, k]), toward(11+2*k, "left", GS.at[1, k], GV.at[0, k]))
        for message in messages:
            start(message)
        return messages

    place(64, C[0, 128:192] + C[1, 0:64])
    place(128, C[0, 192:256] + C[1, 64:128])
    sides = [send_sides(0, 64, 128)]
    wait_recv(gradient_up)
    place(192, C[1, 128:192] + FD[...])
    wait_recv(gradient_down)
    place(0, C[0, 64:128] + FU[...])
    sides.append(send_sides(1, 192, 0))

    for k, (p, q) in enumerate(((64, 128), (192, 0))):
        for message in sides[k]:
            wait_recv(message)
        grad_v[p:p+64] += jnp.where(low, GV[1, k], GV[0, k])
        grad_v[q:q+64] += swap(jnp.where(low, GV[0, k], GV[1, k]))
    gradient_out = pltpu.make_async_copy(grad_v, gradient, local_sem.at[7])
    gradient_out.start()
    for message in (*cols[0], *cols[1], *plain, *corner, gradient_up, gradient_down, *sides[0], *sides[1]):
        wait_send(message)
    aerial_out.wait()
    gradient_out.wait()


def local(mask_field, target, kernel_real, kernel_imag):
    V, H = pltpu.VMEM, pltpu.HBM
    tile = mask_field.shape
    return pl.pallas_call(
        kernel,
        out_shape=(jax.ShapeDtypeStruct(tile, F32),) * 2,
        in_specs=[pl.BlockSpec(memory_space=H)] * 6,
        out_specs=[pl.BlockSpec(memory_space=H)] * 2,
        scratch_shapes=[
            V((2, 384, 128), F32),
            V((256, 128), jnp.int32),
            V((2, 4, 128, 128), F32),
            V(PACKED[0].shape, BF16),
            V(PACKED[1].shape, BF16),
            V((8, 4, 128, 128), F32),
            V((2, 4, 128, 128), F32),
            V((2, 8, 128, 128), F32),
            V((2, 128, 128), F32),
            V((2, 4, 128, 128), F32),
            V((3, 8, 256, 256), BF16),
            V((2, 2, 8, 256, 256), BF16),
            V((2, 2, 8, 128, 256), BF16),
            V((2, 256, 256), F32),
            V((256, 128), F32),
            V((256, 128), F32),
            V((256, 128), F32),
            V((2, 2, 64, 128), F32),
            V((2, 2, 64, 128), F32),
            V((64, 256), F32),
            V((64, 256), F32),
            V((2, 2, 64, 128), F32),
            V((2, 2, 64, 128), F32),
            pltpu.SemaphoreType.DMA((8,)),
            pltpu.SemaphoreType.DMA((14,)),
            pltpu.SemaphoreType.DMA((14,)),
        ],
        compiler_params=pltpu.CompilerParams(vmem_limit_bytes=60 * 2**20, collective_id=0, has_side_effects=True),
        name="litho",
    )(mask_field, target, kernel_real, kernel_imag, *[jnp.asarray(p) for p in PACKED])


def solution(mesh):
    in_specs = (P("row", "col"), P("row", "col"), P(), P())
    out_specs = (P("row", "col"), P("row", "col"))
    return jax.shard_map(local, mesh=mesh, in_specs=in_specs, out_specs=out_specs, check_vma=False)
```

```python
import jax
import jax.numpy as jnp
import numpy as np
from jax import lax
from jax.experimental import pallas as pl
from jax.experimental.pallas import tpu as pltpu
from jax.sharding import PartitionSpec as P

F32, BF16 = jnp.float32, jnp.bfloat16
MESH = pl.DeviceIdType.MESH
steepness = 1.5
threshold = 2.7


def table():
    freq = 2 * np.pi * (np.arange(128) + 0.5) / 256
    col = np.arange(256)
    col = np.where(col < 192, col, col - 256)
    tap = np.arange(128) - 64
    row = np.arange(256)
    both = lambda position, axis: np.concatenate(
        [f(np.outer(position, freq) if axis else np.outer(freq, position)) for f in (np.cos, np.sin)], axis
    )
    back = both(col, 0) * np.repeat([1.0, -1.0], 128)[:, None] / 32768.0
    return np.concatenate([both(tap, 1), both(row, 0), both(col, 1), both(row, 1), back], 0).astype(np.float32)


TABLE = table()
FIRST = 384


def dot(a, b):
    return jnp.dot(a, b, preferred_element_type=F32)


def split(x):
    high = x.astype(BF16)
    return high, (x - high.astype(F32)).astype(BF16)


def lanes(a, b):
    return jnp.concatenate([a, b], axis=1)


def rows(a, b):
    return jnp.concatenate([a, b], axis=0)


def swap(x):
    return pltpu.roll(x, 64, 1)


def butterfly(o):
    cc, cs, sc, ss = o[:128, :128], o[:128, 128:], o[128:, :128], o[128:, 128:]
    return cc - ss, cs + sc, cc + ss, cs - sc


def split_first(tab, t):
    t["wk_hh"][:128], t["wk_l"][...] = split(tab[:128])
    t["wk_hh"][128:] = t["wk_hh"][:128]
    t["cs_h"][...], t["cs_l"][...] = split(tab[128:384])
    t["ca_hh"][:, :128] = t["cs_h"][:, :128]
    t["ca_hh"][:, 128:] = t["cs_h"][:, :128]


def split_second(tab, t):
    t["wm_h"][...], t["wm_l"][...] = split(tab[384:640])
    t["wy_hh"][:128] = t["wm_h"][:128]
    t["wy_hh"][128:] = t["wm_h"][:128]
    t["l2_h"][...], t["l2_l"][...] = split(tab[640:896])
    t["wi_h"][...], t["wi_l"][...] = split(tab[896:1152])
    t["wiy_hl"][:, :128] = t["wi_h"][:, :128]
    t["wiy_hl"][:, 128:] = t["wi_l"][:, :128]


def kernel_spectra(t, k_ref, c_s, H):
    for part in range(2):
        for k in range(4):
            xh, xl = split(k_ref[part, k])
            c = dot(lanes(xh, xl), t["wk_hh"][...]) + dot(xh, t["wk_l"][...])
            c_s[2 * k + part, :128], c_s[2 * k + part, 128:] = split(c)
    for j in range(8):
        o = dot(t["ca_hh"][...], c_s[j]) + dot(t["cs_l"][:, :128], c_s[j, :128])
        for n, v in enumerate(butterfly(o)):
            H[j, n] = v


def mask_spectrum(t, block, M):
    xh, xl = split(block)
    c = dot(xh, t["wm_h"][...]) + dot(xl, t["wm_h"][...]) + dot(xh, t["wm_l"][...])
    ch, cl = split(c)
    o = dot(t["cs_h"][...], ch) + dot(t["cs_h"][...], cl) + dot(t["cs_l"][...], ch)
    for n, v in enumerate(butterfly(o)):
        M[n] = v


def field_rows(t, H, M, d_s, z_s, j):
    def one(n):
        mr, mi, hr, hi = M[n], M[n + 1], H[j, n], H[j, n + 1]
        return mr * hr + mi * hi, mr * hi - mi * hr

    pr, pi = one(0)
    nr, ni = one(2)
    d_s[0, j], d_s[1, j] = split(rows(lanes(pr + nr, pi + ni), lanes(ni - pi, pr - nr)))
    dh, dl = d_s[0, j], d_s[1, j]
    z = dot(t["l2_h"][:128], dh) + dot(t["l2_h"][:128], dl) + dot(t["l2_l"][:128], dh)
    z_s[0, j], z_s[1, j] = split(z)


def field_columns(t, z_s, f, j):
    a = dot(z_s[0, j], t["wiy_hl"][...])
    f[j] = a[:, :128] + a[:, 128:] + dot(z_s[1, j], t["wi_h"][:, :128])


def image(f, target):
    a = f[0] * f[0]
    for j in range(1, 8):
        a = a + f[j] * f[j]
    resist = jax.nn.sigmoid(steepness * (a - threshold))
    return a, 2.0 * (resist - target.astype(F32)) * steepness * resist * (1.0 - resist)


def back_columns(t, f, slope, c_s, j):
    gh, gl = split(slope[...] * f[j])
    c = dot(lanes(gh, gl), t["wy_hh"][...]) + dot(gh, t["wm_l"][:128])
    c_s[j, :128], c_s[j, 128:] = split(c)


def back_rows(t, H, c_s, T, j):
    o = dot(t["ca_hh"][...], c_s[j]) + dot(t["cs_l"][:, :128], c_s[j, :128])
    b = butterfly(o)
    for n in (0, 2):
        gr, gi, hr, hi = b[n], b[n + 1], H[j, n], H[j, n + 1]
        tr, ti = gr * hr - gi * hi, gr * hi + gi * hr
        if j:
            tr, ti = tr + T[n], ti + T[n + 1]
        T[n], T[n + 1] = tr, ti


def final_rows(t, T):
    rp, ip, rm, im = T[0], T[1], T[2], T[3]
    dh, dl = split(2.0 * rows(lanes(rp + rm, -(ip + im)), lanes(ip - im, rp - rm)))
    return split(dot(t["l2_h"][...], dh) + dot(t["l2_h"][...], dl) + dot(t["l2_l"][...], dh))


def final_columns(t, z, which):
    zh, zl = z
    wh, wl = t["wi_h"][:, which], t["wi_l"][:, which]
    return dot(zh, wh) + dot(zl, wh) + dot(zh, wl)


OWN, SIDE = slice(0, 128), slice(128, 256)
SPLITS = dict(
    wk_hh=(256, 256), wk_l=(128, 256), cs_h=(256, 256), cs_l=(256, 256), ca_hh=(256, 256), wm_h=(256, 256),
    wm_l=(256, 256), wy_hh=(256, 256), l2_h=(256, 256), l2_l=(256, 256), wi_h=(256, 256), wi_l=(256, 256),
    wiy_hl=(256, 256),
)


def kernel(mask, target, kr, ki, tab, aerial, gradient,
           E, target_v, k_v, tab_v, H, M, f, slope, T, c_s, d_s, z_s, C, S, aerial_v,
           side_out, side_in, corner_out, corner_in,
           g0_out, g0_in, g1_out, g1_in, gc_out, gc_in, gr_in, local_sem, send_sem, recv_sem, *splits):
    t = dict(zip(SPLITS, splits))
    r, c = lax.axis_index("row"), lax.axis_index("col")
    nr, nc = lax.axis_size("row"), lax.axis_size("col")
    near = {"u": r > 0, "d": r < nr - 1, "l": c > 0, "r": c < nc - 1}
    shift = {"u": (-1, 0), "d": (1, 0), "l": (0, -1), "r": (0, 1)}
    opposite = {"u": "d", "d": "u", "l": "r", "r": "l"}

    def there(way):
        cond = near[way[0]]
        for w in way[1:]:
            cond = jnp.logical_and(cond, near[w])
        return cond

    def device(way):
        return (r + sum(shift[w][0] for w in way), c + sum(shift[w][1] for w in way))

    local = []
    for n, (src, dst) in enumerate(((mask, E.at[0, pl.ds(64, 256)]), (kr, k_v.at[0]), (ki, k_v.at[1]),
                                    (tab.at[pl.ds(0, FIRST)], tab_v.at[pl.ds(0, FIRST)]),
                                    (tab.at[pl.ds(FIRST, 768)], tab_v.at[pl.ds(FIRST, 768)]), (target, target_v))):
        local.append(pltpu.make_async_copy(src, dst, local_sem.at[n]))
        local[-1].start()

    ways = ("l", "r", "u", "d", "ul", "ur", "dl", "dr")
    barrier = pltpu.get_barrier_semaphore()
    for way in ways:
        @pl.when(there(way))
        def _():
            pl.semaphore_signal(barrier, inc=1, device_id=device(way), device_id_type=MESH)

    def empty(way, *refs):
        @pl.when(jnp.logical_not(there(way)))
        def _():
            for ref in refs:
                ref[...] = jnp.zeros(ref.shape, F32)

    place = {"l": 0, "r": 1}
    for way in "lr":
        n = 1 - place[way]
        empty(way, side_in.at[:, n], g0_in.at[n], g1_in.at[n])
        empty("u" + way, corner_in.at[0, n], gc_in.at[0, n])
        empty("d" + way, corner_in.at[1, n], gc_in.at[1, n])
    empty("u", E.at[0, pl.ds(0, 64)], gr_in.at[0])
    empty("d", E.at[0, pl.ds(320, 64)], gr_in.at[1])

    sent = []

    def message(way, src, dst):
        n = len(sent)
        copy = pltpu.make_async_remote_copy(src_ref=src, dst_ref=dst, send_sem=send_sem.at[n], recv_sem=recv_sem.at[n],
                                            device_id=device(way), device_id_type=MESH)
        sent.append((copy, way))

        @pl.when(there(way))
        def _():
            copy.start()

        return copy, "".join(opposite[w] for w in way)

    def arrive(*messages):
        for copy, come in messages:
            @pl.when(there(come))
            def _(copy=copy):
                copy.wait_recv()

    def is_low(n):
        return lax.broadcasted_iota(jnp.int32, (n, 128), 1) < 64

    def pack(ref, first, second, low_place=0):
        low, second = is_low(first.shape[0]), swap(second)
        ref[low_place] = jnp.where(low, first, second)
        ref[1 - low_place] = jnp.where(low, second, first)

    local[0].wait()
    for k in range(2):
        pack(side_out.at[k], E[0, 64 + 128 * k : 128 + 128 * k], E[0, 128 + 128 * k : 192 + 128 * k])
    pack(corner_out.at[0], E[0, 256:288], E[0, 288:320])
    pack(corner_out.at[1], E[0, 64:96], E[0, 96:128])
    pl.semaphore_wait(barrier, sum(there(way).astype(jnp.int32) for way in ways))
    sides = [[message(way, side_out.at[0, place[way]], side_in.at[0, place[way]]) for way in "lr"]]
    above = [message("d" + way, corner_out.at[0, place[way]], corner_in.at[0, place[way]]) for way in "lr"]
    sides.append([message(way, side_out.at[1, place[way]], side_in.at[1, place[way]]) for way in "lr"])
    above.append(message("d", E.at[0, pl.ds(256, 64)], E.at[0, pl.ds(0, 64)]))
    below = [message("u" + way, corner_out.at[1, place[way]], corner_in.at[1, place[way]]) for way in "lr"]
    below.append(message("u", E.at[0, pl.ds(64, 64)], E.at[0, pl.ds(320, 64)]))

    local[3].wait()
    split_first(tab_v, t)
    local[1].wait()
    local[2].wait()
    kernel_spectra(t, k_v, c_s.at[0], H)
    local[4].wait()
    split_second(tab_v, t)
    local[5].wait()

    def unpack(ref, start):
        n = ref.shape[1]
        low, from_right, from_left = is_low(n), ref[0], ref[1]
        E[1, start : start + n] = jnp.where(low, from_right, from_left)
        E[1, start + n : start + 2 * n] = swap(jnp.where(low, from_left, from_right))

    arrive(*sides[0], *sides[1], *above)
    unpack(side_in.at[0], 64)
    unpack(side_in.at[1], 192)
    unpack(corner_in.at[0], 0)
    mask_spectrum(t, lanes(E[0, :256], E[1, :256]), M.at[0])
    for j in range(8):
        field_rows(t, H, M.at[0], d_s.at[0], z_s.at[0], j)
    for j in range(8):
        field_columns(t, z_s.at[0], f.at[0], j)
    aerial_v[:128], slope[0] = image(f.at[0], target_v[:128])
    arrive(*below)
    unpack(corner_in.at[1], 320)
    mask_spectrum(t, lanes(E[0, 128:], E[1, 128:]), M.at[1])
    for j in range(8):
        back_columns(t, f.at[0], slope.at[0], c_s.at[1], j)
        field_rows(t, H, M.at[1], d_s.at[1], z_s.at[1], j)
    for j in range(8):
        back_rows(t, H, c_s.at[1], T.at[0], j)
        field_columns(t, z_s.at[1], f.at[1], j)
    aerial_v[128:], slope[1] = image(f.at[1], target_v[128:])
    aerial_out = pltpu.make_async_copy(aerial_v, aerial, local_sem.at[6])
    aerial_out.start()
    z = final_rows(t, T.at[0])
    S[0] = final_columns(t, z, SIDE)
    pack(gc_out.at[0], S[0, 0:32], S[0, 32:64], 1)
    pack(g0_out, S[0, 64:96], S[0, 96:128], 1)
    C[0] = final_columns(t, z, OWN)
    early = [message("u" + way, gc_out.at[0, place[way]], gc_in.at[1, place[way]]) for way in "lr"]
    early += [message(way, g0_out.at[place[way]], g0_in.at[place[way]]) for way in "lr"]
    early.append(message("u", C.at[0, pl.ds(0, 64)], gr_in.at[1]))
    for j in range(8):
        back_columns(t, f.at[1], slope.at[1], c_s.at[2], j)
    for j in range(8):
        back_rows(t, H, c_s.at[2], T.at[1], j)
    z = final_rows(t, T.at[1])
    S[1] = final_columns(t, z, SIDE)
    middle = S[0, 128:256] + S[1, 0:128]
    pack(g1_out, middle[:96], rows(middle[96:], S[1, 128:192]), 1)
    pack(gc_out.at[1], S[1, 192:224], S[1, 224:256], 1)
    late = [message(way, g1_out.at[place[way]], g1_in.at[place[way]]) for way in "lr"]
    late += [message("d" + way, gc_out.at[1, place[way]], gc_in.at[0, place[way]]) for way in "lr"]
    C[1] = final_columns(t, z, OWN)
    late.append(message("d", C.at[1, pl.ds(192, 64)], gr_in.at[0]))
    own = rows(C[0, 64:256], C[1, 128:192])
    own = rows(own[:64], rows(own[64:192] + C[1, 0:128], own[192:]))

    def gain(ref):
        low, from_right, from_left = is_low(ref.shape[1]), ref[0], ref[1]
        return rows(jnp.where(low, from_left, from_right), swap(jnp.where(low, from_right, from_left)))

    arrive(*early)
    arrive(*late)
    add = rows(gain(g0_in), gain(g1_in))
    add = rows(add[:64] + gain(gc_in.at[0]) + gr_in[0], rows(add[64:192], add[192:] + gain(gc_in.at[1]) + gr_in[1]))
    S[0, :256] = own + add
    gradient_out = pltpu.make_async_copy(S.at[0], gradient, local_sem.at[7])
    gradient_out.start()
    for copy, way in sent:
        @pl.when(there(way))
        def _():
            copy.wait_send()
    aerial_out.wait()
    gradient_out.wait()


def hand_over(first, second, first_out, second_out, buf, sem):
    ins = [pltpu.make_async_copy(src, buf.at[n], sem.at[n]) for n, src in enumerate((first, second))]
    outs = [pltpu.make_async_copy(buf.at[n], dst, sem.at[2 + n]) for n, dst in enumerate((first_out, second_out))]
    for copy in ins:
        copy.start()
    for copy, out in zip(ins, outs):
        copy.wait()
        out.start()
    for out in outs:
        out.wait()


def local(mask_field, target, kernel_real, kernel_imag):
    V, HBM = pltpu.VMEM, pltpu.HBM
    tile = jax.ShapeDtypeStruct(mask_field.shape, F32)
    results = pl.pallas_call(
        kernel,
        out_shape=(tile, tile),
        in_specs=[pl.BlockSpec(memory_space=HBM)] * 5,
        out_specs=[pl.BlockSpec(memory_space=HBM)] * 2,
        scratch_shapes=[
            V((2, 384, 128), F32),
            V((256, 128), jnp.int32),
            V((2, 4, 128, 128), F32),
            V(TABLE.shape, F32),
            V((8, 4, 128, 128), F32),
            V((2, 4, 128, 128), F32),
            V((2, 8, 128, 128), F32),
            V((2, 128, 128), F32),
            V((2, 4, 128, 128), F32),
            V((3, 8, 256, 256), BF16),
            V((2, 2, 8, 256, 256), BF16),
            V((2, 2, 8, 128, 256), BF16),
            V((2, 256, 128), F32),
            V((2, 256, 128), F32),
            V((256, 128), F32),
            V((2, 2, 64, 128), F32),
            V((2, 2, 64, 128), F32),
            V((2, 2, 32, 128), F32),
            V((2, 2, 32, 128), F32),
            V((2, 32, 128), F32),
            V((2, 32, 128), F32),
            V((2, 96, 128), F32),
            V((2, 96, 128), F32),
            V((2, 2, 32, 128), F32),
            V((2, 2, 32, 128), F32),
            V((2, 64, 128), F32),
            pltpu.SemaphoreType.DMA((8,)),
            pltpu.SemaphoreType.DMA((20,)),
            pltpu.SemaphoreType.DMA((20,)),
        ] + [V(shape, BF16) for shape in SPLITS.values()],
        compiler_params=pltpu.CompilerParams(vmem_limit_bytes=60 * 2**20, collective_id=0, has_side_effects=True),
        name="litho",
    )(mask_field, target, kernel_real, kernel_imag, jnp.asarray(TABLE))
    return pl.pallas_call(
        hand_over,
        out_shape=(tile, tile),
        in_specs=[pl.BlockSpec(memory_space=HBM)] * 2,
        out_specs=[pl.BlockSpec(memory_space=HBM)] * 2,
        scratch_shapes=[V((2, 256, 128), F32), pltpu.SemaphoreType.DMA((4,))],
        name="hand_over",
    )(*results)


def solution(mesh):
    in_specs = (P("row", "col"), P("row", "col"), P(), P())
    out_specs = (P("row", "col"), P("row", "col"))
    return jax.shard_map(local, mesh=mesh, in_specs=in_specs, out_specs=out_specs, check_vma=False)
```

```python
import jax
import jax.numpy as jnp
import numpy as np
from jax import lax
from jax.experimental import pallas as pl
from jax.experimental.pallas import tpu as pltpu
from jax.sharding import PartitionSpec as P

F32, BF16 = jnp.float32, jnp.bfloat16
MESH = pl.DeviceIdType.MESH
steepness = 1.5
threshold = 2.7


def table():
    freq = 2 * np.pi * (np.arange(128) + 0.5) / 256
    col = np.arange(256)
    col = np.where(col < 192, col, col - 256)
    tap = np.arange(128) - 64
    row = np.arange(256)
    both = lambda position, axis: np.concatenate(
        [f(np.outer(position, freq) if axis else np.outer(freq, position)) for f in (np.cos, np.sin)], axis
    )
    back = both(col, 0) * np.repeat([1.0, -1.0], 128)[:, None] / 32768.0
    return np.concatenate([both(tap, 1), both(row, 0), both(col, 1), both(row, 1), back], 0).astype(np.float32)


TABLE = table()
FIRST = 384


def dot(a, b):
    return jnp.dot(a, b, preferred_element_type=F32)


def split(x):
    high = x.astype(BF16)
    return high, (x - high.astype(F32)).astype(BF16)


def lanes(a, b):
    return jnp.concatenate([a, b], axis=1)


def rows(a, b):
    return jnp.concatenate([a, b], axis=0)


def swap(x):
    return pltpu.roll(x, 64, 1)


def butterfly(o):
    cc, cs, sc, ss = o[:128, :128], o[:128, 128:], o[128:, :128], o[128:, 128:]
    return cc - ss, cs + sc, cc + ss, cs - sc


def split_first(tab, t):
    t["wk_hh"][:128], t["wk_l"][...] = split(tab[:128])
    t["wk_hh"][128:] = t["wk_hh"][:128]
    t["cs_h"][...], t["cs_l"][...] = split(tab[128:384])
    t["ca_hh"][:, :128] = t["cs_h"][:, :128]
    t["ca_hh"][:, 128:] = t["cs_h"][:, :128]


def split_second(tab, t):
    t["wm_h"][...], t["wm_l"][...] = split(tab[384:640])
    t["wy_hh"][:128] = t["wm_h"][:128]
    t["wy_hh"][128:] = t["wm_h"][:128]
    t["l2_h"][...], t["l2_l"][...] = split(tab[640:896])
    t["wi_h"][...], t["wi_l"][...] = split(tab[896:1152])
    t["wiy_hl"][:, :128] = t["wi_h"][:, :128]
    t["wiy_hl"][:, 128:] = t["wi_l"][:, :128]


def kernel_spectra(t, k_ref, c_s, H):
    for part in range(2):
        for k in range(4):
            xh, xl = split(k_ref[part, k])
            c = dot(lanes(xh, xl), t["wk_hh"][...]) + dot(xh, t["wk_l"][...])
            c_s[2 * k + part, :128], c_s[2 * k + part, 128:] = split(c)
    for j in range(8):
        o = dot(t["ca_hh"][...], c_s[j]) + dot(t["cs_l"][:, :128], c_s[j, :128])
        for n, v in enumerate(butterfly(o)):
            H[j, n] = v


def mask_spectrum(t, block, M):
    xh, xl = split(block)
    c = dot(xh, t["wm_h"][...]) + dot(xl, t["wm_h"][...]) + dot(xh, t["wm_l"][...])
    ch, cl = split(c)
    o = dot(t["cs_h"][...], ch) + dot(t["cs_h"][...], cl) + dot(t["cs_l"][...], ch)
    for n, v in enumerate(butterfly(o)):
        M[n] = v


def field_rows(t, H, M, d_s, z_s, j):
    def one(n):
        mr, mi, hr, hi = M[n], M[n + 1], H[j, n], H[j, n + 1]
        return mr * hr + mi * hi, mr * hi - mi * hr

    pr, pi = one(0)
    nr, ni = one(2)
    d_s[0, j], d_s[1, j] = split(rows(lanes(pr + nr, pi + ni), lanes(ni - pi, pr - nr)))
    dh, dl = d_s[0, j], d_s[1, j]
    z = dot(t["l2_h"][:128], dh) + dot(t["l2_h"][:128], dl) + dot(t["l2_l"][:128], dh)
    z_s[0, j], z_s[1, j] = split(z)


def field_columns(t, z_s, f, j):
    a = dot(z_s[0, j], t["wiy_hl"][...])
    f[j] = a[:, :128] + a[:, 128:] + dot(z_s[1, j], t["wi_h"][:, :128])


def image(f, target):
    a = f[0] * f[0]
    for j in range(1, 8):
        a = a + f[j] * f[j]
    resist = jax.nn.sigmoid(steepness * (a - threshold))
    return a, 2.0 * (resist - target.astype(F32)) * steepness * resist * (1.0 - resist)


def back_columns(t, f, slope, c_s, j):
    gh, gl = split(slope[...] * f[j])
    c = dot(lanes(gh, gl), t["wy_hh"][...]) + dot(gh, t["wm_l"][:128])
    c_s[j, :128], c_s[j, 128:] = split(c)


def back_rows(t, H, c_s, T, j):
    o = dot(t["ca_hh"][...], c_s[j]) + dot(t["cs_l"][:, :128], c_s[j, :128])
    b = butterfly(o)
    for n in (0, 2):
        gr, gi, hr, hi = b[n], b[n + 1], H[j, n], H[j, n + 1]
        tr, ti = gr * hr - gi * hi, gr * hi + gi * hr
        if j:
            tr, ti = tr + T[n], ti + T[n + 1]
        T[n], T[n + 1] = tr, ti


def final_rows(t, T):
    rp, ip, rm, im = T[0], T[1], T[2], T[3]
    dh, dl = split(2.0 * rows(lanes(rp + rm, -(ip + im)), lanes(ip - im, rp - rm)))
    return split(dot(t["l2_h"][...], dh) + dot(t["l2_h"][...], dl) + dot(t["l2_l"][...], dh))


def final_columns(t, z, which):
    zh, zl = z
    wh, wl = t["wi_h"][:, which], t["wi_l"][:, which]
    return dot(zh, wh) + dot(zl, wh) + dot(zh, wl)


OWN, SIDE = slice(0, 128), slice(128, 256)
SPLITS = dict(
    wk_hh=(256, 256), wk_l=(128, 256), cs_h=(256, 256), cs_l=(256, 256), ca_hh=(256, 256), wm_h=(256, 256),
    wm_l=(256, 256), wy_hh=(256, 256), l2_h=(256, 256), l2_l=(256, 256), wi_h=(256, 256), wi_l=(256, 256),
    wiy_hl=(256, 256),
)


def kernel(mask, target, kr, ki, tab, aerial, gradient,
           E, target_v, k_v, tab_v, H, M, f, slope, T, c_s, d_s, z_s, C, S, aerial_v, grad_v,
           side_out, side_in, corner_out, corner_in,
           g0_out, g0_in, g1_out, g1_in, gc_out, gc_in, gr_in, local_sem, send_sem, recv_sem, ready, *splits):
    t = dict(zip(SPLITS, splits))
    r, c = lax.axis_index("row"), lax.axis_index("col")
    nr, nc = lax.axis_size("row"), lax.axis_size("col")
    near = {"u": r > 0, "d": r < nr - 1, "l": c > 0, "r": c < nc - 1}
    shift = {"u": (-1, 0), "d": (1, 0), "l": (0, -1), "r": (0, 1)}
    opposite = {"u": "d", "d": "u", "l": "r", "r": "l"}

    def there(way):
        cond = near[way[0]]
        for w in way[1:]:
            cond = jnp.logical_and(cond, near[w])
        return cond

    def device(way):
        return (r + sum(shift[w][0] for w in way), c + sum(shift[w][1] for w in way))

    local = []
    for n, (src, dst) in enumerate(((mask, E.at[0, pl.ds(64, 256)]), (kr, k_v.at[0]), (ki, k_v.at[1]),
                                    (tab.at[pl.ds(0, FIRST)], tab_v.at[pl.ds(0, FIRST)]),
                                    (tab.at[pl.ds(FIRST, 768)], tab_v.at[pl.ds(FIRST, 768)]), (target, target_v))):
        local.append(pltpu.make_async_copy(src, dst, local_sem.at[n]))
        local[-1].start()

    ways = ("l", "r", "u", "d", "ul", "ur", "dl", "dr")
    barrier = pltpu.get_barrier_semaphore()
    z = lax.rem(r, 8)
    opens, closes = z == 0, z == 7
    for way in ways:
        tells = jnp.logical_and(there(way), jnp.logical_not(closes)) if way[0] == "d" else there(way)
        @pl.when(tells)
        def _():
            pl.semaphore_signal(barrier, inc=1, device_id=device(way), device_id_type=MESH)

    def empty(way, *refs):
        @pl.when(jnp.logical_not(there(way)))
        def _():
            for ref in refs:
                ref[...] = jnp.zeros(ref.shape, F32)

    place = {"l": 0, "r": 1}
    for way in "lr":
        n = 1 - place[way]
        empty(way, side_in.at[:, n], g0_in.at[n], g1_in.at[n])
        empty("u" + way, corner_in.at[0, n], gc_in.at[0, n])
        empty("d" + way, corner_in.at[1, n], gc_in.at[1, n])
    empty("u", E.at[0, pl.ds(0, 64)], gr_in.at[0])
    empty("d", E.at[0, pl.ds(320, 64)], gr_in.at[1])

    lower = jnp.logical_or(opens, closes)
    upper = jnp.logical_not(lower)
    first = lower.astype(jnp.int32)
    second = 1 - first

    sent = []

    def message(way, src, dst):
        n = len(sent)
        copy = pltpu.make_async_remote_copy(src_ref=src, dst_ref=dst, send_sem=send_sem.at[n], recv_sem=recv_sem.at[n],
                                            device_id=device(way), device_id_type=MESH)
        sent.append((copy, way))
        return copy, way

    def start(messages, now=None):
        for copy, way in messages:
            go = there(way)
            @pl.when(go if now is None else jnp.logical_and(go, now))
            def _(copy=copy):
                copy.start()

    def arrive(messages, now=None):
        for copy, way in messages:
            come = there("".join(opposite[w] for w in way))
            @pl.when(come if now is None else jnp.logical_and(come, now))
            def _(copy=copy):
                copy.wait_recv()

    def is_low(n):
        return lax.broadcasted_iota(jnp.int32, (n, 128), 1) < 64

    def pack(ref, first, second, low_place=0):
        low, second = is_low(first.shape[0]), swap(second)
        ref[low_place] = jnp.where(low, first, second)
        ref[1 - low_place] = jnp.where(low, second, first)

    def both(src, dst, toward=""):
        return [message(toward + way, src.at[place[way]], dst.at[place[way]]) for way in "lr"]

    side = [both(side_out.at[k], side_in.at[k]) for k in range(2)]
    to_below = both(corner_out.at[0], corner_in.at[0], "d") + [
        message("d", E.at[0, pl.ds(256, 64)], E.at[0, pl.ds(0, 64)])]
    to_above = both(corner_out.at[1], corner_in.at[1], "u") + [
        message("u", E.at[0, pl.ds(64, 64)], E.at[0, pl.ds(320, 64)])]
    out_above = both(gc_out.at[0], gc_in.at[1], "u") + [message("u", C.at[first, pl.ds(0, 64)], gr_in.at[1])]
    out_below = both(gc_out.at[1], gc_in.at[0], "d") + [message("d", C.at[second, pl.ds(192, 64)], gr_in.at[0])]
    out_edge = both(g0_out, g0_in)
    out_rest = both(g1_out, g1_in)

    local[0].wait()
    for k in range(2):
        pack(side_out.at[k], E[0, 64 + 128 * k : 128 + 128 * k], E[0, 128 + 128 * k : 192 + 128 * k])
    pack(corner_out.at[0], E[0, 256:288], E[0, 288:320])
    pack(corner_out.at[1], E[0, 64:96], E[0, 96:128])
    def heard(way):
        return jnp.logical_and(there(way), jnp.logical_not(opens)) if way[0] == "u" else there(way)

    pl.semaphore_wait(barrier, sum(heard(way).astype(jnp.int32) for way in ways))
    for k, way in enumerate(("d", "dl", "dr")):
        @pl.when(jnp.logical_and(there(way), closes))
        def _():
            pl.semaphore_signal(ready.at[k], inc=1, device_id=device(way), device_id_type=MESH)

    start(side[0] + side[1] + to_below)
    start(to_above, jnp.logical_not(opens))

    local[3].wait()
    split_first(tab_v, t)
    local[1].wait()
    local[2].wait()
    kernel_spectra(t, k_v, c_s.at[0], H)
    local[4].wait()
    split_second(tab_v, t)
    local[5].wait()

    def unpack(ref, begin):
        n = ref.shape[1]
        low, from_right, from_left = is_low(n), ref[0], ref[1]
        E[1, pl.ds(begin, n)] = jnp.where(low, from_right, from_left)
        E[1, pl.ds(begin + n, n)] = swap(jnp.where(low, from_left, from_right))

    def spectrum(n, b):
        unpack(corner_in.at[b], pl.multiple_of(320 * b, 64))
        span = pl.ds(pl.multiple_of(128 * b, 128), 256)
        mask_spectrum(t, lanes(E[0, span], E[1, span]), M.at[n])

    def expose(n, b):
        span = pl.ds(pl.multiple_of(128 * b, 128), 128)
        aerial_v[span], slope[n] = image(f.at[n], target_v[span])

    def outer(b):
        return pl.multiple_of(192 * b, 64)

    def edge(b):
        return pl.multiple_of(64 + 64 * b, 64)

    def pack_outer(n, b):
        start_row = outer(b)
        pack(gc_out.at[b], S[n, pl.ds(start_row, 32)], S[n, pl.ds(start_row + 32, 32)], 1)

    for odd in (1, 0):
        for (copy, way), k in zip(to_above, (2, 1, 0)):
            column = c + sum(shift[w][1] for w in way)
            @pl.when(jnp.logical_and(jnp.logical_and(there(way), opens), lax.rem(lax.div(column, 2), 2) == odd))
            def _(copy=copy, k=k):
                pl.semaphore_wait(ready.at[k], 1)
                copy.start()

    arrive(side[0] + side[1])
    arrive(to_below, upper)
    arrive(to_above, lower)
    unpack(side_in.at[0], 64)
    unpack(side_in.at[1], 192)
    spectrum(0, first)
    for j in range(8):
        field_rows(t, H, M.at[0], d_s.at[0], z_s.at[0], j)
    for j in range(8):
        field_columns(t, z_s.at[0], f.at[0], j)
    expose(0, first)
    for j in range(8):
        back_columns(t, f.at[0], slope.at[0], c_s.at[1], j)
    for j in range(8):
        back_rows(t, H, c_s.at[1], T.at[0], j)
    zz = final_rows(t, T.at[0])
    S[0] = final_columns(t, zz, SIDE)
    pack_outer(0, first)
    edge_row = edge(first)
    pack(g0_out, S[0, pl.ds(edge_row, 32)], S[0, pl.ds(edge_row + 32, 32)], 1)
    C[0] = final_columns(t, zz, OWN)
    start(out_above, upper)
    start(out_below, lower)
    start(out_edge)
    arrive(to_below, lower)
    arrive(to_above, upper)
    spectrum(1, second)
    for j in range(8):
        field_rows(t, H, M.at[1], d_s.at[1], z_s.at[1], j)
    for j in range(8):
        field_columns(t, z_s.at[1], f.at[1], j)
    expose(1, second)
    aerial_out = pltpu.make_async_copy(aerial_v, aerial, local_sem.at[6])
    aerial_out.start()
    for j in range(8):
        back_columns(t, f.at[1], slope.at[1], c_s.at[2], j)
    for j in range(8):
        back_rows(t, H, c_s.at[2], T.at[1], j)
    zz = final_rows(t, T.at[1])
    S[1] = final_columns(t, zz, SIDE)
    pack_outer(1, second)
    middle = S[first, 128:256] + S[second, 0:128]
    pack(g1_out, middle[:96], rows(middle[96:], S[1, pl.ds(edge(second), 64)]), 1)
    C[1] = final_columns(t, zz, OWN)
    start(out_rest)
    start(out_above, lower)
    start(out_below, upper)
    grad_v[:64] = C[first, 64:128]
    grad_v[64:192] = C[first, 128:256] + C[second, 0:128]
    grad_v[192:] = C[second, 128:192]

    def gain(ref):
        low, from_right, from_left = is_low(ref.shape[1]), ref[0], ref[1]
        return rows(jnp.where(low, from_left, from_right), swap(jnp.where(low, from_right, from_left)))

    arrive(out_edge + out_rest + out_above + out_below)
    rest = gain(g1_in)
    grad_v[64:192] += rest[:128]
    grad_v[pl.ds(pl.multiple_of(192 * second, 64), 64)] += rest[128:]
    grad_v[pl.ds(pl.multiple_of(192 * first, 64), 64)] += gain(g0_in)
    grad_v[:64] += gain(gc_in.at[0]) + gr_in[0]
    grad_v[192:] += gain(gc_in.at[1]) + gr_in[1]
    gradient_out = pltpu.make_async_copy(grad_v, gradient, local_sem.at[7])
    gradient_out.start()
    for copy, way in sent:
        @pl.when(there(way))
        def _():
            copy.wait_send()
    aerial_out.wait()
    gradient_out.wait()


def hand_over(first, second, first_out, second_out, buf, sem):
    ins = [pltpu.make_async_copy(src, buf.at[n], sem.at[n]) for n, src in enumerate((first, second))]
    outs = [pltpu.make_async_copy(buf.at[n], dst, sem.at[2 + n]) for n, dst in enumerate((first_out, second_out))]
    for copy in ins:
        copy.start()
    for copy, out in zip(ins, outs):
        copy.wait()
        out.start()
    for out in outs:
        out.wait()


def local(mask_field, target, kernel_real, kernel_imag):
    V, HBM = pltpu.VMEM, pltpu.HBM
    tile = jax.ShapeDtypeStruct(mask_field.shape, F32)
    results = pl.pallas_call(
        kernel,
        out_shape=(tile, tile),
        in_specs=[pl.BlockSpec(memory_space=HBM)] * 5,
        out_specs=[pl.BlockSpec(memory_space=HBM)] * 2,
        scratch_shapes=[
            V((2, 384, 128), F32),
            V((256, 128), jnp.int32),
            V((2, 4, 128, 128), F32),
            V(TABLE.shape, F32),
            V((8, 4, 128, 128), F32),
            V((2, 4, 128, 128), F32),
            V((2, 8, 128, 128), F32),
            V((2, 128, 128), F32),
            V((2, 4, 128, 128), F32),
            V((3, 8, 256, 256), BF16),
            V((2, 2, 8, 256, 256), BF16),
            V((2, 2, 8, 128, 256), BF16),
            V((2, 256, 128), F32),
            V((2, 256, 128), F32),
            V((256, 128), F32),
            V((256, 128), F32),
            V((2, 2, 64, 128), F32),
            V((2, 2, 64, 128), F32),
            V((2, 2, 32, 128), F32),
            V((2, 2, 32, 128), F32),
            V((2, 32, 128), F32),
            V((2, 32, 128), F32),
            V((2, 96, 128), F32),
            V((2, 96, 128), F32),
            V((2, 2, 32, 128), F32),
            V((2, 2, 32, 128), F32),
            V((2, 64, 128), F32),
            pltpu.SemaphoreType.DMA((8,)),
            pltpu.SemaphoreType.DMA((20,)),
            pltpu.SemaphoreType.DMA((20,)),
            pltpu.SemaphoreType.REGULAR((3,)),
        ] + [V(shape, BF16) for shape in SPLITS.values()],
        compiler_params=pltpu.CompilerParams(vmem_limit_bytes=60 * 2**20, collective_id=0, has_side_effects=True),
        name="litho",
    )(mask_field, target, kernel_real, kernel_imag, jnp.asarray(TABLE))
    return pl.pallas_call(
        hand_over,
        out_shape=(tile, tile),
        in_specs=[pl.BlockSpec(memory_space=HBM)] * 2,
        out_specs=[pl.BlockSpec(memory_space=HBM)] * 2,
        scratch_shapes=[V((2, 256, 128), F32), pltpu.SemaphoreType.DMA((4,))],
        name="hand_over",
    )(*results)


def solution(mesh):
    in_specs = (P("row", "col"), P("row", "col"), P(), P())
    out_specs = (P("row", "col"), P("row", "col"))
    return jax.shard_map(local, mesh=mesh, in_specs=in_specs, out_specs=out_specs, check_vma=False)
```

```python
import jax
import jax.numpy as jnp
import numpy as np
from jax import lax
from jax.experimental import pallas as pl
from jax.experimental.pallas import tpu as pltpu
from jax.sharding import PartitionSpec as P

F32, BF16 = jnp.float32, jnp.bfloat16
MESH = pl.DeviceIdType.MESH
steepness = 1.5
threshold = 2.7


def table():
    freq = 2 * np.pi * (np.arange(128) + 0.5) / 256
    col = np.arange(256)
    col = np.where(col < 192, col, col - 256)
    tap = np.arange(128) - 64
    row = np.arange(256)
    both = lambda position, axis: np.concatenate(
        [f(np.outer(position, freq) if axis else np.outer(freq, position)) for f in (np.cos, np.sin)], axis
    )
    back = both(col, 0) * np.repeat([1.0, -1.0], 128)[:, None] / 32768.0
    return np.concatenate([both(tap, 1), both(row, 0), both(col, 1), both(row, 1), back], 0).astype(np.float32)


TABLE = table()
FIRST = 384


def dot(a, b):
    return jnp.dot(a, b, preferred_element_type=F32)


def split(x):
    high = x.astype(BF16)
    return high, (x - high.astype(F32)).astype(BF16)


def lanes(a, b):
    return jnp.concatenate([a, b], axis=1)


def rows(a, b):
    return jnp.concatenate([a, b], axis=0)


def swap(x):
    return pltpu.roll(x, 64, 1)


def butterfly(o):
    cc, cs, sc, ss = o[:128, :128], o[:128, 128:], o[128:, :128], o[128:, 128:]
    return cc - ss, cs + sc, cc + ss, cs - sc


def split_first(tab, t):
    t["wk_hh"][:128], t["wk_l"][...] = split(tab[:128])
    t["wk_hh"][128:] = t["wk_hh"][:128]
    t["cs_h"][...], t["cs_l"][...] = split(tab[128:384])
    t["ca_hh"][:, :128] = t["cs_h"][:, :128]
    t["ca_hh"][:, 128:] = t["cs_h"][:, :128]


def split_second(tab, t):
    t["wm_h"][...], t["wm_l"][...] = split(tab[384:640])
    t["wy_hh"][:128] = t["wm_h"][:128]
    t["wy_hh"][128:] = t["wm_h"][:128]
    t["l2_h"][...], t["l2_l"][...] = split(tab[640:896])
    t["wi_h"][...], t["wi_l"][...] = split(tab[896:1152])
    t["wiy_hl"][:, :128] = t["wi_h"][:, :128]
    t["wiy_hl"][:, 128:] = t["wi_l"][:, :128]


def kernel_spectra(t, k_ref, c_s, H):
    for part in range(2):
        for k in range(4):
            xh, xl = split(k_ref[part, k])
            c = dot(lanes(xh, xl), t["wk_hh"][...]) + dot(xh, t["wk_l"][...])
            c_s[2 * k + part, :128], c_s[2 * k + part, 128:] = split(c)
    for j in range(8):
        o = dot(t["ca_hh"][...], c_s[j]) + dot(t["cs_l"][:, :128], c_s[j, :128])
        for n, v in enumerate(butterfly(o)):
            H[j, n] = v


def mask_spectrum(t, block, M):
    xh, xl = split(block)
    c = dot(xh, t["wm_h"][...]) + dot(xl, t["wm_h"][...]) + dot(xh, t["wm_l"][...])
    ch, cl = split(c)
    o = dot(t["cs_h"][...], ch) + dot(t["cs_h"][...], cl) + dot(t["cs_l"][...], ch)
    for n, v in enumerate(butterfly(o)):
        M[n] = v


def field_rows(t, H, M, d_s, z_s, j):
    def one(n):
        mr, mi, hr, hi = M[n], M[n + 1], H[j, n], H[j, n + 1]
        return mr * hr + mi * hi, mr * hi - mi * hr

    pr, pi = one(0)
    nr, ni = one(2)
    d_s[0, j], d_s[1, j] = split(rows(lanes(pr + nr, pi + ni), lanes(ni - pi, pr - nr)))
    dh, dl = d_s[0, j], d_s[1, j]
    z = dot(t["l2_h"][:128], dh) + dot(t["l2_h"][:128], dl) + dot(t["l2_l"][:128], dh)
    z_s[0, j], z_s[1, j] = split(z)


def field_columns(t, z_s, f, j):
    a = dot(z_s[0, j], t["wiy_hl"][...])
    f[j] = a[:, :128] + a[:, 128:] + dot(z_s[1, j], t["wi_h"][:, :128])


def image(f, target):
    a = f[0] * f[0]
    for j in range(1, 8):
        a = a + f[j] * f[j]
    resist = jax.nn.sigmoid(steepness * (a - threshold))
    return a, 2.0 * (resist - target.astype(F32)) * steepness * resist * (1.0 - resist)


def back_columns(t, f, slope, c_s, j):
    gh, gl = split(slope[...] * f[j])
    c = dot(lanes(gh, gl), t["wy_hh"][...]) + dot(gh, t["wm_l"][:128])
    c_s[j, :128], c_s[j, 128:] = split(c)


def back_rows(t, H, c_s, T, j):
    o = dot(t["ca_hh"][...], c_s[j]) + dot(t["cs_l"][:, :128], c_s[j, :128])
    b = butterfly(o)
    for n in (0, 2):
        gr, gi, hr, hi = b[n], b[n + 1], H[j, n], H[j, n + 1]
        tr, ti = gr * hr - gi * hi, gr * hi + gi * hr
        if j:
            tr, ti = tr + T[n], ti + T[n + 1]
        T[n], T[n + 1] = tr, ti


def final_rows(t, T):
    rp, ip, rm, im = T[0], T[1], T[2], T[3]
    dh, dl = split(2.0 * rows(lanes(rp + rm, -(ip + im)), lanes(ip - im, rp - rm)))
    return split(dot(t["l2_h"][...], dh) + dot(t["l2_h"][...], dl) + dot(t["l2_l"][...], dh))


def final_columns(t, z, which):
    zh, zl = z
    wh, wl = t["wi_h"][:, which], t["wi_l"][:, which]
    return dot(zh, wh) + dot(zl, wh) + dot(zh, wl)


OWN, SIDE = slice(0, 128), slice(128, 256)
SPLITS = dict(
    wk_hh=(256, 256), wk_l=(128, 256), cs_h=(256, 256), cs_l=(256, 256), ca_hh=(256, 256), wm_h=(256, 256),
    wm_l=(256, 256), wy_hh=(256, 256), l2_h=(256, 256), l2_l=(256, 256), wi_h=(256, 256), wi_l=(256, 256),
    wiy_hl=(256, 256),
)


def lower_first(r):
    z = lax.rem(r, 8)
    return jnp.logical_or(z == 0, z == 7)


def kernel(mask, target, kr, ki, tab, aerial, partial, g0_in, g1_in, gc_in, gr_in,
           E, target_v, k_v, tab_v, H, M, f, slope, T, c_s, d_s, z_s, C, S, aerial_v, grad_v,
           side_out, side_in, edge_in, corner_out, corner_in,
           g0_out, g1_out, gc_out, local_sem, send_sem, recv_sem, ready, *splits):
    t = dict(zip(SPLITS, splits))
    r, c = lax.axis_index("row"), lax.axis_index("col")
    nr, nc = lax.axis_size("row"), lax.axis_size("col")
    near = {"u": r > 0, "d": r < nr - 1, "l": c > 0, "r": c < nc - 1}
    shift = {"u": (-1, 0), "d": (1, 0), "l": (0, -1), "r": (0, 1)}
    opposite = {"u": "d", "d": "u", "l": "r", "r": "l"}

    def there(way):
        cond = near[way[0]]
        for w in way[1:]:
            cond = jnp.logical_and(cond, near[w])
        return cond

    def device(way):
        return (r + sum(shift[w][0] for w in way), c + sum(shift[w][1] for w in way))

    local = []
    for n, (src, dst) in enumerate(((mask, E.at[0, pl.ds(64, 256)]), (kr, k_v.at[0]), (ki, k_v.at[1]),
                                    (tab.at[pl.ds(0, FIRST)], tab_v.at[pl.ds(0, FIRST)]),
                                    (tab.at[pl.ds(FIRST, 768)], tab_v.at[pl.ds(FIRST, 768)]), (target, target_v))):
        local.append(pltpu.make_async_copy(src, dst, local_sem.at[n]))
        local[-1].start()

    ways = ("l", "r", "u", "d", "ul", "ur", "dl", "dr")
    barrier = pltpu.get_barrier_semaphore()
    z = lax.rem(r, 8)
    opens, closes = z == 0, z == 7
    inner_up, inner_down = jnp.logical_and(near["u"], jnp.logical_not(opens)), jnp.logical_and(near["d"], jnp.logical_not(closes))
    ways = ("l", "r", "u", "d", "ul", "ur", "dl", "dr")
    tells = {"l": near["l"], "r": near["r"], "u": near["u"], "d": inner_down,
             "ul": jnp.logical_and(opens, there("ul")), "ur": jnp.logical_and(opens, there("ur"))}
    hears = {"l": near["l"], "r": near["r"], "u": inner_up, "d": near["d"],
             "dl": jnp.logical_and(closes, there("dl")), "dr": jnp.logical_and(closes, there("dr"))}
    barrier = pltpu.get_barrier_semaphore()
    for way, cond in tells.items():
        @pl.when(cond)
        def _():
            pl.semaphore_signal(barrier, inc=1, device_id=device(way), device_id_type=MESH)

    def word(sem, way, cond):
        @pl.when(cond)
        def _():
            pl.semaphore_signal(sem, inc=1, device_id=device(way), device_id_type=MESH)

    def hear(sem, cond):
        @pl.when(cond)
        def _():
            pl.semaphore_wait(sem, 1)

    def empty(way, *refs):
        @pl.when(jnp.logical_not(there(way)))
        def _():
            for ref in refs:
                ref[...] = jnp.zeros(ref.shape, F32)

    place = {"l": 0, "r": 1}
    for way in "lr":
        n = 1 - place[way]
        empty(way, side_in.at[n], edge_in.at[:, n])
        empty("u" + way, corner_in.at[0, n])
        empty("d" + way, corner_in.at[1, n])
    empty("u", E.at[0, pl.ds(0, 64)])
    empty("d", E.at[0, pl.ds(320, 64)])

    lower = lower_first(r)
    upper = jnp.logical_not(lower)
    first = lower.astype(jnp.int32)
    second = 1 - first

    sent = []

    def message(way, src, dst):
        n = len(sent)
        copy = pltpu.make_async_remote_copy(src_ref=src, dst_ref=dst, send_sem=send_sem.at[n], recv_sem=recv_sem.at[n],
                                            device_id=device(way), device_id_type=MESH)
        sent.append((copy, way))
        return copy, way

    def start(messages, now=None):
        for copy, way in messages:
            go = there(way)
            @pl.when(go if now is None else jnp.logical_and(go, now))
            def _(copy=copy):
                copy.start()

    def arrive(messages, now=None):
        for copy, way in messages:
            come = there("".join(opposite[w] for w in way))
            @pl.when(come if now is None else jnp.logical_and(come, now))
            def _(copy=copy):
                copy.wait_recv()

    def is_low(n):
        return lax.broadcasted_iota(jnp.int32, (n, 128), 1) < 64

    def pack(ref, first, second, low_place=0):
        low, second = is_low(first.shape[0]), swap(second)
        ref[low_place] = jnp.where(low, first, second)
        ref[1 - low_place] = jnp.where(low, second, first)

    def both(src, dst, toward=""):
        return [message(toward + way, src.at[place[way]], dst.at[place[way]]) for way in "lr"]

    side = both(side_out, side_in)
    edges = [both(corner_out.at[1 - k], edge_in.at[k]) for k in range(2)]
    to_below = both(corner_out.at[0], corner_in.at[0], "d") + [
        message("d", E.at[0, pl.ds(256, 64)], E.at[0, pl.ds(0, 64)])]
    to_above = both(corner_out.at[1], corner_in.at[1], "u") + [
        message("u", E.at[0, pl.ds(64, 64)], E.at[0, pl.ds(320, 64)])]
    corner_above, row_above = both(gc_out.at[0], gc_in.at[1], "u"), [message("u", C.at[first, pl.ds(0, 64)], gr_in.at[1])]
    corner_below, row_below = both(gc_out.at[1], gc_in.at[0], "d"), [message("d", C.at[second, pl.ds(192, 64)], gr_in.at[0])]
    out_edge = both(g0_out, g0_in)
    out_rest = both(g1_out, g1_in)

    local[0].wait()
    pack(side_out, E[0, 128:192], E[0, 192:256])
    pack(corner_out.at[0], E[0, 256:288], E[0, 288:320])
    pack(corner_out.at[1], E[0, 64:96], E[0, 96:128])
    pl.semaphore_wait(barrier, sum(cond.astype(jnp.int32) for cond in hears.values()))
    word(ready.at[0], "d", jnp.logical_and(closes, near["d"]))
    word(ready.at[1], "d", inner_down)
    word(ready.at[2], "u", inner_up)
    start(to_below, closes)
    start(side)
    start(edges[0], upper)
    start(edges[1], lower)
    start(to_below[2:], jnp.logical_not(closes))
    start(to_above[2:], jnp.logical_not(opens))
    start(edges[1], upper)
    start(edges[0], lower)

    local[3].wait()
    split_first(tab_v, t)
    local[1].wait()
    local[2].wait()
    kernel_spectra(t, k_v, c_s.at[0], H)
    hear(ready.at[2], inner_down)
    start(to_below[:2], jnp.logical_not(closes))
    hear(ready.at[1], inner_up)
    start(to_above[:2], jnp.logical_not(opens))
    local[4].wait()
    split_second(tab_v, t)
    local[5].wait()

    def unpack(ref, begin):
        n = ref.shape[1]
        low, from_right, from_left = is_low(n), ref[0], ref[1]
        E[1, pl.ds(begin, n)] = jnp.where(low, from_right, from_left)
        E[1, pl.ds(begin + n, n)] = swap(jnp.where(low, from_left, from_right))

    def spectrum(n, b):
        unpack(corner_in.at[b], pl.multiple_of(320 * b, 64))
        unpack(edge_in.at[b], pl.multiple_of(64 + 192 * b, 64))
        span = pl.ds(pl.multiple_of(128 * b, 128), 256)
        mask_spectrum(t, lanes(E[0, span], E[1, span]), M.at[n])

    def expose(n, b):
        span = pl.ds(pl.multiple_of(128 * b, 128), 128)
        aerial_v[span], slope[n] = image(f.at[n], target_v[span])

    def outer(b):
        return pl.multiple_of(192 * b, 64)

    def edge(b):
        return pl.multiple_of(64 + 64 * b, 64)

    def pack_outer(n, b):
        start_row = outer(b)
        pack(gc_out.at[b], S[n, pl.ds(start_row, 32)], S[n, pl.ds(start_row + 32, 32)], 1)

    hear(ready.at[0], jnp.logical_and(opens, near["u"]))
    start(to_above, opens)

    arrive(side)
    arrive(edges[0] + to_below, upper)
    arrive(edges[1] + to_above, lower)
    unpack(side_in, 128)
    spectrum(0, first)
    for j in range(8):
        field_rows(t, H, M.at[0], d_s.at[0], z_s.at[0], j)
    for j in range(8):
        field_columns(t, z_s.at[0], f.at[0], j)
    expose(0, first)
    for j in range(8):
        back_columns(t, f.at[0], slope.at[0], c_s.at[1], j)
    for j in range(8):
        back_rows(t, H, c_s.at[1], T.at[0], j)
    zz = final_rows(t, T.at[0])
    S[0] = final_columns(t, zz, SIDE)
    pack_outer(0, first)
    edge_row = edge(first)
    pack(g0_out, S[0, pl.ds(edge_row, 32)], S[0, pl.ds(edge_row + 32, 32)], 1)
    start(corner_above, upper)
    start(corner_below, lower)
    start(out_edge)
    C[0] = final_columns(t, zz, OWN)
    start(row_above, upper)
    start(row_below, lower)
    arrive(edges[0] + to_below, lower)
    arrive(edges[1] + to_above, upper)
    spectrum(1, second)
    for j in range(8):
        field_rows(t, H, M.at[1], d_s.at[1], z_s.at[1], j)
    for j in range(8):
        field_columns(t, z_s.at[1], f.at[1], j)
    expose(1, second)
    aerial_out = pltpu.make_async_copy(aerial_v, aerial, local_sem.at[6])
    aerial_out.start()
    for j in range(8):
        back_columns(t, f.at[1], slope.at[1], c_s.at[2], j)
    for j in range(8):
        back_rows(t, H, c_s.at[2], T.at[1], j)
    zz = final_rows(t, T.at[1])
    S[1] = final_columns(t, zz, SIDE)
    pack_outer(1, second)
    middle = S[first, 128:256] + S[second, 0:128]
    pack(g1_out, middle[:96], rows(middle[96:], S[1, pl.ds(edge(second), 64)]), 1)
    start(out_rest)
    start(corner_above, lower)
    start(corner_below, upper)
    C[1] = final_columns(t, zz, OWN)
    start(row_above, lower)
    start(row_below, upper)
    grad_v[:64] = C[first, 64:128]
    grad_v[64:192] = C[first, 128:256] + C[second, 0:128]
    grad_v[192:] = C[second, 128:192]

    partial_out = pltpu.make_async_copy(grad_v, partial, local_sem.at[7])
    partial_out.start()
    arrive(out_edge + out_rest + corner_above + corner_below + row_above + row_below)
    for copy, way in sent:
        @pl.when(there(way))
        def _():
            copy.wait_send()
    aerial_out.wait()
    partial_out.wait()


def add_up(aerial, partial, g0, g1, gc, gr, aerial_out, gradient_out,
           aerial_v, grad_v, g0_v, g1_v, gc_v, gr_v, sem):
    ins = [pltpu.make_async_copy(src, dst, sem.at[n]) for n, (src, dst) in enumerate((
        (aerial, aerial_v), (partial, grad_v), (g0, g0_v), (g1, g1_v), (gc, gc_v), (gr, gr_v)))]
    for copy in ins:
        copy.start()
    r, c = lax.axis_index("row"), lax.axis_index("col")
    nr, nc = lax.axis_size("row"), lax.axis_size("col")
    up, down, left, right = r > 0, r < nr - 1, c > 0, c < nc - 1
    first = lower_first(r).astype(jnp.int32)

    def gain(ref, cond=None):
        from_right, from_left = ref[0], ref[1]
        here_right = right if cond is None else jnp.logical_and(right, cond)
        here_left = left if cond is None else jnp.logical_and(left, cond)
        from_right = jnp.where(here_right, from_right, 0.0)
        from_left = jnp.where(here_left, from_left, 0.0)
        low = lax.broadcasted_iota(jnp.int32, from_left.shape, 1) < 64
        return rows(jnp.where(low, from_left, from_right), swap(jnp.where(low, from_right, from_left)))

    ins[0].wait()
    aerial_copy = pltpu.make_async_copy(aerial_v, aerial_out, sem.at[6])
    aerial_copy.start()
    for copy in ins[1:]:
        copy.wait()
    rest = gain(g1_v)
    grad_v[64:192] += rest[:128]
    grad_v[pl.ds(pl.multiple_of(192 * (1 - first), 64), 64)] += rest[128:]
    grad_v[pl.ds(pl.multiple_of(192 * first, 64), 64)] += gain(g0_v)
    grad_v[:64] += gain(gc_v.at[0], up) + jnp.where(up, gr_v[0], 0.0)
    grad_v[192:] += gain(gc_v.at[1], down) + jnp.where(down, gr_v[1], 0.0)
    gradient_copy = pltpu.make_async_copy(grad_v, gradient_out, sem.at[7])
    gradient_copy.start()
    aerial_copy.wait()
    gradient_copy.wait()


def local(mask_field, target, kernel_real, kernel_imag):
    V, HBM = pltpu.VMEM, pltpu.HBM
    tile = jax.ShapeDtypeStruct(mask_field.shape, F32)
    landing = tuple(jax.ShapeDtypeStruct(shape, F32) for shape in ((2, 32, 128), (2, 96, 128), (2, 2, 32, 128), (2, 64, 128)))
    results = pl.pallas_call(
        kernel,
        out_shape=(tile, tile) + landing,
        in_specs=[pl.BlockSpec(memory_space=HBM)] * 5,
        out_specs=[pl.BlockSpec(memory_space=HBM)] * 6,
        scratch_shapes=[
            V((2, 384, 128), F32),
            V((256, 128), jnp.int32),
            V((2, 4, 128, 128), F32),
            V(TABLE.shape, F32),
            V((8, 4, 128, 128), F32),
            V((2, 4, 128, 128), F32),
            V((2, 8, 128, 128), F32),
            V((2, 128, 128), F32),
            V((2, 4, 128, 128), F32),
            V((3, 8, 256, 256), BF16),
            V((2, 2, 8, 256, 256), BF16),
            V((2, 2, 8, 128, 256), BF16),
            V((2, 256, 128), F32),
            V((2, 256, 128), F32),
            V((256, 128), F32),
            V((256, 128), F32),
            V((2, 64, 128), F32),
            V((2, 64, 128), F32),
            V((2, 2, 32, 128), F32),
            V((2, 2, 32, 128), F32),
            V((2, 2, 32, 128), F32),
            V((2, 32, 128), F32),
            V((2, 96, 128), F32),
            V((2, 2, 32, 128), F32),
            pltpu.SemaphoreType.DMA((8,)),
            pltpu.SemaphoreType.DMA((22,)),
            pltpu.SemaphoreType.DMA((22,)),
            pltpu.SemaphoreType.REGULAR((3,)),
        ] + [V(shape, BF16) for shape in SPLITS.values()],
        compiler_params=pltpu.CompilerParams(vmem_limit_bytes=60 * 2**20, collective_id=0, has_side_effects=True),
        name="litho",
    )(mask_field, target, kernel_real, kernel_imag, jnp.asarray(TABLE))
    return pl.pallas_call(
        add_up,
        out_shape=(tile, tile),
        in_specs=[pl.BlockSpec(memory_space=HBM)] * 6,
        out_specs=[pl.BlockSpec(memory_space=HBM)] * 2,
        scratch_shapes=[V(tile.shape, F32)] * 2 + [V(x.shape, F32) for x in landing] + [pltpu.SemaphoreType.DMA((8,))],
        name="add_up",
    )(*results)


def solution(mesh):
    in_specs = (P("row", "col"), P("row", "col"), P(), P())
    out_specs = (P("row", "col"), P("row", "col"))
    return jax.shard_map(local, mesh=mesh, in_specs=in_specs, out_specs=out_specs, check_vma=False)
```

```python
import jax
import jax.numpy as jnp
import numpy as np
from jax import lax
from jax.experimental import pallas as pl
from jax.experimental.pallas import tpu as pltpu
from jax.sharding import PartitionSpec as P

F32, BF16 = jnp.float32, jnp.bfloat16
MESH = pl.DeviceIdType.MESH
steepness = 1.5
threshold = 2.7


def table():
    freq = 2 * np.pi * (np.arange(128) + 0.5) / 256
    col = np.arange(256)
    col = np.where(col < 192, col, col - 256)
    tap = np.arange(128) - 64
    row = np.arange(256)
    both = lambda position, axis: np.concatenate(
        [f(np.outer(position, freq) if axis else np.outer(freq, position)) for f in (np.cos, np.sin)], axis
    )
    back = both(col, 0) * np.repeat([1.0, -1.0], 128)[:, None] / 32768.0
    return np.concatenate([both(tap, 1), both(row, 0), both(col, 1), both(row, 1), back], 0).astype(np.float32)


TABLE = table()
FIRST = 384


def dot(a, b):
    return jnp.dot(a, b, preferred_element_type=F32)


def split(x):
    high = x.astype(BF16)
    return high, (x - high.astype(F32)).astype(BF16)


def lanes(a, b):
    return jnp.concatenate([a, b], axis=1)


def rows(a, b):
    return jnp.concatenate([a, b], axis=0)


def swap(x):
    return pltpu.roll(x, 64, 1)


def butterfly(o):
    cc, cs, sc, ss = o[:128, :128], o[:128, 128:], o[128:, :128], o[128:, 128:]
    return cc - ss, cs + sc, cc + ss, cs - sc


def split_first(tab, t):
    t["wk_hh"][:128], t["wk_l"][...] = split(tab[:128])
    t["wk_hh"][128:] = t["wk_hh"][:128]
    t["cs_h"][...], t["cs_l"][...] = split(tab[128:384])
    t["ca_hh"][:, :128] = t["cs_h"][:, :128]
    t["ca_hh"][:, 128:] = t["cs_h"][:, :128]


def split_second(tab, t):
    t["wm_h"][...], t["wm_l"][...] = split(tab[384:640])
    t["wy_hh"][:128] = t["wm_h"][:128]
    t["wy_hh"][128:] = t["wm_h"][:128]
    t["l2_h"][...], t["l2_l"][...] = split(tab[640:896])
    t["wi_h"][...], t["wi_l"][...] = split(tab[896:1152])
    t["wiy_hl"][:, :128] = t["wi_h"][:, :128]
    t["wiy_hl"][:, 128:] = t["wi_l"][:, :128]


def kernel_spectra(t, k_ref, c_s, H):
    for part in range(2):
        for k in range(4):
            xh, xl = split(k_ref[part, k])
            c = dot(lanes(xh, xl), t["wk_hh"][...]) + dot(xh, t["wk_l"][...])
            c_s[2 * k + part, :128], c_s[2 * k + part, 128:] = split(c)
    for j in range(8):
        o = dot(t["ca_hh"][...], c_s[j]) + dot(t["cs_l"][:, :128], c_s[j, :128])
        for n, v in enumerate(butterfly(o)):
            H[j, n] = v


def mask_spectrum(t, block, M):
    xh, xl = split(block)
    c = dot(xh, t["wm_h"][...]) + dot(xl, t["wm_h"][...]) + dot(xh, t["wm_l"][...])
    ch, cl = split(c)
    o = dot(t["cs_h"][...], ch) + dot(t["cs_h"][...], cl) + dot(t["cs_l"][...], ch)
    for n, v in enumerate(butterfly(o)):
        M[n] = v


def field_rows(t, H, M, d_s, z_s, j):
    def one(n):
        mr, mi, hr, hi = M[n], M[n + 1], H[j, n], H[j, n + 1]
        return mr * hr + mi * hi, mr * hi - mi * hr

    pr, pi = one(0)
    nr, ni = one(2)
    d_s[0, j], d_s[1, j] = split(rows(lanes(pr + nr, pi + ni), lanes(ni - pi, pr - nr)))
    dh, dl = d_s[0, j], d_s[1, j]
    z = dot(t["l2_h"][:128], dh) + dot(t["l2_h"][:128], dl) + dot(t["l2_l"][:128], dh)
    z_s[0, j], z_s[1, j] = split(z)


def field_columns(t, z_s, f, j):
    a = dot(z_s[0, j], t["wiy_hl"][...])
    f[j] = a[:, :128] + a[:, 128:] + dot(z_s[1, j], t["wi_h"][:, :128])


def image(f, target):
    a = f[0] * f[0]
    for j in range(1, 8):
        a = a + f[j] * f[j]
    resist = jax.nn.sigmoid(steepness * (a - threshold))
    return a, 2.0 * (resist - target.astype(F32)) * steepness * resist * (1.0 - resist)


def back_columns(t, f, slope, c_s, j):
    gh, gl = split(slope[...] * f[j])
    c = dot(lanes(gh, gl), t["wy_hh"][...]) + dot(gh, t["wm_l"][:128])
    c_s[j, :128], c_s[j, 128:] = split(c)


def back_rows(t, H, c_s, T, j):
    o = dot(t["ca_hh"][...], c_s[j]) + dot(t["cs_l"][:, :128], c_s[j, :128])
    b = butterfly(o)
    for n in (0, 2):
        gr, gi, hr, hi = b[n], b[n + 1], H[j, n], H[j, n + 1]
        tr, ti = gr * hr - gi * hi, gr * hi + gi * hr
        if j:
            tr, ti = tr + T[n], ti + T[n + 1]
        T[n], T[n + 1] = tr, ti


def final_rows(t, T):
    rp, ip, rm, im = T[0], T[1], T[2], T[3]
    dh, dl = split(2.0 * rows(lanes(rp + rm, -(ip + im)), lanes(ip - im, rp - rm)))
    return split(dot(t["l2_h"][...], dh) + dot(t["l2_h"][...], dl) + dot(t["l2_l"][...], dh))


def final_columns(t, z, which):
    zh, zl = z
    wh, wl = t["wi_h"][:, which], t["wi_l"][:, which]
    return dot(zh, wh) + dot(zl, wh) + dot(zh, wl)


OWN, SIDE = slice(0, 128), slice(128, 256)
SPLITS = dict(
    wk_hh=(256, 256), wk_l=(128, 256), cs_h=(256, 256), cs_l=(256, 256), ca_hh=(256, 256), wm_h=(256, 256),
    wm_l=(256, 256), wy_hh=(256, 256), l2_h=(256, 256), l2_l=(256, 256), wi_h=(256, 256), wi_l=(256, 256),
    wiy_hl=(256, 256),
)


def lower_first(r):
    z = lax.rem(r, 8)
    return jnp.logical_or(z == 0, z == 7)


def kernel(mask, target, kr, ki, tab, aerial, partial, g0_in, g1_in, gc_in, gr_in,
           E, target_v, k_v, tab_v, H, M, f, slope, T, c_s, d_s, z_s, C, S, aerial_v, grad_v,
           side_out, side_in, edge_in, corner_out, corner_in,
           g0_out, g1_out, gc_out, local_sem, send_sem, recv_sem, ready, *splits):
    t = dict(zip(SPLITS, splits))
    r, c = lax.axis_index("row"), lax.axis_index("col")
    nr, nc = lax.axis_size("row"), lax.axis_size("col")
    near = {"u": r > 0, "d": r < nr - 1, "l": c > 0, "r": c < nc - 1}
    shift = {"u": (-1, 0), "d": (1, 0), "l": (0, -1), "r": (0, 1)}
    opposite = {"u": "d", "d": "u", "l": "r", "r": "l"}

    def there(way):
        cond = near[way[0]]
        for w in way[1:]:
            cond = jnp.logical_and(cond, near[w])
        return cond

    def device(way):
        return (r + sum(shift[w][0] for w in way), c + sum(shift[w][1] for w in way))

    local = []
    for n, (src, dst) in enumerate(((mask, E.at[0, pl.ds(64, 256)]), (kr, k_v.at[0]), (ki, k_v.at[1]),
                                    (tab.at[pl.ds(0, FIRST)], tab_v.at[pl.ds(0, FIRST)]),
                                    (tab.at[pl.ds(FIRST, 768)], tab_v.at[pl.ds(FIRST, 768)]), (target, target_v))):
        local.append(pltpu.make_async_copy(src, dst, local_sem.at[n]))
        local[-1].start()

    z = lax.rem(r, 8)
    opens, closes = z == 0, z == 7
    both_hold = jnp.logical_and
    inner_up, inner_down = both_hold(near["u"], jnp.logical_not(opens)), both_hold(near["d"], jnp.logical_not(closes))
    outer_up, outer_down = both_hold(near["u"], opens), both_hold(near["d"], closes)
    odd = lax.rem(lax.div(c, 2), 2) == 1
    across = {"l": both_hold(closes, lax.rem(c, 2) == 0), "r": both_hold(closes, lax.rem(c, 2) == 1)}
    late_here = {way: both_hold(both_hold(near[way], across[way]), odd) for way in "lr"}
    late_there = {way: both_hold(both_hold(near[way], across[way]), jnp.logical_not(odd)) for way in "lr"}
    tells = {"l": both_hold(near["l"], jnp.logical_not(late_here["l"])),
             "r": both_hold(near["r"], jnp.logical_not(late_here["r"])), "u": near["u"], "d": inner_down,
             "ul": both_hold(opens, there("ul")), "ur": both_hold(opens, there("ur"))}
    hears = {"l": both_hold(near["l"], jnp.logical_not(late_there["l"])),
             "r": both_hold(near["r"], jnp.logical_not(late_there["r"])), "u": inner_up, "d": near["d"],
             "dl": both_hold(closes, there("dl")), "dr": both_hold(closes, there("dr"))}
    barrier = pltpu.get_barrier_semaphore()
    for way, cond in tells.items():
        @pl.when(cond)
        def _():
            pl.semaphore_signal(barrier, inc=1, device_id=device(way), device_id_type=MESH)

    def word(sem, way, cond):
        @pl.when(cond)
        def _():
            pl.semaphore_signal(sem, inc=1, device_id=device(way), device_id_type=MESH)

    def hear(sem, cond):
        @pl.when(cond)
        def _():
            pl.semaphore_wait(sem, 1)

    def empty(way, *refs):
        @pl.when(jnp.logical_not(there(way)))
        def _():
            for ref in refs:
                ref[...] = jnp.zeros(ref.shape, F32)

    place = {"l": 0, "r": 1}
    for way in "lr":
        n = 1 - place[way]
        empty(way, side_in.at[n], edge_in.at[:, n])
        empty("u" + way, corner_in.at[n])
    empty("u", E.at[:, pl.ds(0, 64)])
    empty("d", E.at[:, pl.ds(320, 64)])

    lower = lower_first(r)
    upper = jnp.logical_not(lower)
    first = lower.astype(jnp.int32)
    second = 1 - first

    sent = []

    def message(way, src, dst, if_sent=None, if_taken=None):
        n = len(sent)
        copy = pltpu.make_async_remote_copy(src_ref=src, dst_ref=dst, send_sem=send_sem.at[n], recv_sem=recv_sem.at[n],
                                            device_id=device(way), device_id_type=MESH)
        go, come = there(way), there("".join(opposite[w] for w in way))
        go = go if if_sent is None else both_hold(go, if_sent)
        come = come if if_taken is None else both_hold(come, if_taken)
        sent.append((copy, go, come))
        return sent[-1]

    def start(messages, now=None):
        for copy, go, _ in messages:
            @pl.when(go if now is None else both_hold(go, now))
            def _(copy=copy):
                copy.start()

    def arrive(messages, now=None):
        for copy, _, come in messages:
            @pl.when(come if now is None else both_hold(come, now))
            def _(copy=copy):
                copy.wait_recv()

    def is_low(n):
        return lax.broadcasted_iota(jnp.int32, (n, 128), 1) < 64

    def pack(ref, first, second, low_place=0):
        low, second = is_low(first.shape[0]), swap(second)
        ref[low_place] = jnp.where(low, first, second)
        ref[1 - low_place] = jnp.where(low, second, first)

    def both(src, dst, toward="", **when):
        return [message(toward + way, src.at[place[way]], dst.at[place[way]], **when) for way in "lr"]

    side = both(side_out, side_in)
    edges = [both(corner_out.at[1 - k], edge_in.at[k]) for k in range(2)]
    corners = both(corner_out.at[0], corner_in, "d", if_sent=closes, if_taken=opens)
    rows_down = [message("d", E.at[0, pl.ds(256, 64)], E.at[0, pl.ds(0, 64)])]
    rows_up = [message("u", E.at[0, pl.ds(64, 64)], E.at[0, pl.ds(320, 64)])]
    relay_down = [message("d", E.at[1, pl.ds(256, 64)], E.at[1, pl.ds(0, 64)], jnp.logical_not(closes), jnp.logical_not(opens))]
    relay_up = [message("u", E.at[1, pl.ds(64, 64)], E.at[1, pl.ds(320, 64)])]
    from_above = rows_down + relay_down + corners
    from_below = rows_up + relay_up
    corner_above, row_above = both(gc_out.at[0], gc_in.at[1], "u"), [message("u", C.at[first, pl.ds(0, 64)], gr_in.at[1])]
    corner_below, row_below = both(gc_out.at[1], gc_in.at[0], "d"), [message("d", C.at[second, pl.ds(192, 64)], gr_in.at[0])]
    out_edge = both(g0_out, g0_in)
    out_rest = both(g1_out, g1_in)

    local[0].wait()
    pack(side_out, E[0, 128:192], E[0, 192:256])
    pack(corner_out.at[0], E[0, 256:288], E[0, 288:320])
    pack(corner_out.at[1], E[0, 64:96], E[0, 96:128])
    pl.semaphore_wait(barrier, sum(cond.astype(jnp.int32) for cond in hears.values()))
    word(ready.at[0], "d", outer_down)
    for way in "lr":
        word(ready.at[1 + place[way]], way, late_here[way])
    start(corners + rows_down)
    start(rows_up, jnp.logical_not(opens))
    for group in (edges[0], edges[1], side):
        for way in "lr":
            start([group[place[way]]], jnp.logical_not(late_there[way]))

    local[3].wait()
    split_first(tab_v, t)
    local[1].wait()
    local[2].wait()
    kernel_spectra(t, k_v, c_s.at[0], H)
    local[4].wait()
    split_second(tab_v, t)
    local[5].wait()

    def unpack(ref, begin):
        n = ref.shape[1]
        low, from_right, from_left = is_low(n), ref[0], ref[1]
        E[1, pl.ds(begin, n)] = jnp.where(low, from_right, from_left)
        E[1, pl.ds(begin + n, n)] = swap(jnp.where(low, from_left, from_right))

    def spectrum(n, b):
        span = pl.ds(pl.multiple_of(128 * b, 128), 256)
        mask_spectrum(t, lanes(E[0, span], E[1, span]), M.at[n])

    def expose(n, b):
        span = pl.ds(pl.multiple_of(128 * b, 128), 128)
        aerial_v[span], slope[n] = image(f.at[n], target_v[span])

    def outer(b):
        return pl.multiple_of(192 * b, 64)

    def edge(b):
        return pl.multiple_of(64 + 64 * b, 64)

    def pack_outer(n, b):
        start_row = outer(b)
        pack(gc_out.at[b], S[n, pl.ds(start_row, 32)], S[n, pl.ds(start_row + 32, 32)], 1)

    for way in "lr":
        n = place[way]
        hear(ready.at[2 - n], late_there[way])
        start([edges[1][n], side[n], edges[0][n]], late_there[way])
    arrive(edges[0] + edges[1])
    unpack(edge_in.at[0], 64)
    unpack(edge_in.at[1], 256)
    start(relay_down)
    start(relay_up, jnp.logical_not(opens))
    hear(ready.at[0], outer_up)
    start(rows_up + relay_up, opens)
    arrive(side)
    unpack(side_in, 128)
    arrive(from_above, upper)
    arrive(from_below, lower)
    spectrum(0, first)
    for j in range(8):
        field_rows(t, H, M.at[0], d_s.at[0], z_s.at[0], j)
    for j in range(8):
        field_columns(t, z_s.at[0], f.at[0], j)
    expose(0, first)
    for j in range(8):
        back_columns(t, f.at[0], slope.at[0], c_s.at[1], j)
    for j in range(8):
        back_rows(t, H, c_s.at[1], T.at[0], j)
    zz = final_rows(t, T.at[0])
    S[0] = final_columns(t, zz, SIDE)
    pack_outer(0, first)
    edge_row = edge(first)
    pack(g0_out, S[0, pl.ds(edge_row, 32)], S[0, pl.ds(edge_row + 32, 32)], 1)
    start(corner_above, upper)
    start(corner_below, lower)
    start(out_edge)
    C[0] = final_columns(t, zz, OWN)
    start(row_above, upper)
    start(row_below, lower)
    arrive(from_above, lower)
    arrive(from_below, upper)

    @pl.when(opens)
    def _():
        unpack(corner_in, 0)

    spectrum(1, second)
    for j in range(8):
        field_rows(t, H, M.at[1], d_s.at[1], z_s.at[1], j)
    for j in range(8):
        field_columns(t, z_s.at[1], f.at[1], j)
    expose(1, second)
    aerial_out = pltpu.make_async_copy(aerial_v, aerial, local_sem.at[6])
    aerial_out.start()
    for j in range(8):
        back_columns(t, f.at[1], slope.at[1], c_s.at[2], j)
    for j in range(8):
        back_rows(t, H, c_s.at[2], T.at[1], j)
    zz = final_rows(t, T.at[1])
    S[1] = final_columns(t, zz, SIDE)
    pack_outer(1, second)
    middle = S[first, 128:256] + S[second, 0:128]
    pack(g1_out, middle[:96], rows(middle[96:], S[1, pl.ds(edge(second), 64)]), 1)
    start(out_rest)
    start(corner_above, lower)
    start(corner_below, upper)
    C[1] = final_columns(t, zz, OWN)
    start(row_above, lower)
    start(row_below, upper)
    grad_v[:64] = C[first, 64:128]
    grad_v[64:192] = C[first, 128:256] + C[second, 0:128]
    grad_v[192:] = C[second, 128:192]

    partial_out = pltpu.make_async_copy(grad_v, partial, local_sem.at[7])
    partial_out.start()
    arrive(out_edge + out_rest + corner_above + corner_below + row_above + row_below)
    for copy, go, _ in sent:
        @pl.when(go)
        def _():
            copy.wait_send()
    aerial_out.wait()
    partial_out.wait()


def add_up(aerial, partial, g0, g1, gc, gr, aerial_out, gradient_out,
           aerial_v, grad_v, g0_v, g1_v, gc_v, gr_v, sem):
    ins = [pltpu.make_async_copy(src, dst, sem.at[n]) for n, (src, dst) in enumerate((
        (aerial, aerial_v), (partial, grad_v), (g0, g0_v), (g1, g1_v), (gc, gc_v), (gr, gr_v)))]
    for copy in ins:
        copy.start()
    r, c = lax.axis_index("row"), lax.axis_index("col")
    nr, nc = lax.axis_size("row"), lax.axis_size("col")
    up, down, left, right = r > 0, r < nr - 1, c > 0, c < nc - 1
    first = lower_first(r).astype(jnp.int32)

    def gain(ref, cond=None):
        from_right, from_left = ref[0], ref[1]
        here_right = right if cond is None else jnp.logical_and(right, cond)
        here_left = left if cond is None else jnp.logical_and(left, cond)
        from_right = jnp.where(here_right, from_right, 0.0)
        from_left = jnp.where(here_left, from_left, 0.0)
        low = lax.broadcasted_iota(jnp.int32, from_left.shape, 1) < 64
        return rows(jnp.where(low, from_left, from_right), swap(jnp.where(low, from_right, from_left)))

    ins[0].wait()
    aerial_copy = pltpu.make_async_copy(aerial_v, aerial_out, sem.at[6])
    aerial_copy.start()
    for copy in ins[1:]:
        copy.wait()
    rest = gain(g1_v)
    grad_v[64:192] += rest[:128]
    grad_v[pl.ds(pl.multiple_of(192 * (1 - first), 64), 64)] += rest[128:]
    grad_v[pl.ds(pl.multiple_of(192 * first, 64), 64)] += gain(g0_v)
    grad_v[:64] += gain(gc_v.at[0], up) + jnp.where(up, gr_v[0], 0.0)
    grad_v[192:] += gain(gc_v.at[1], down) + jnp.where(down, gr_v[1], 0.0)
    gradient_copy = pltpu.make_async_copy(grad_v, gradient_out, sem.at[7])
    gradient_copy.start()
    aerial_copy.wait()
    gradient_copy.wait()


def local(mask_field, target, kernel_real, kernel_imag):
    V, HBM = pltpu.VMEM, pltpu.HBM
    tile = jax.ShapeDtypeStruct(mask_field.shape, F32)
    landing = tuple(jax.ShapeDtypeStruct(shape, F32) for shape in ((2, 32, 128), (2, 96, 128), (2, 2, 32, 128), (2, 64, 128)))
    results = pl.pallas_call(
        kernel,
        out_shape=(tile, tile) + landing,
        in_specs=[pl.BlockSpec(memory_space=HBM)] * 5,
        out_specs=[pl.BlockSpec(memory_space=HBM)] * 6,
        scratch_shapes=[
            V((2, 384, 128), F32),
            V((256, 128), jnp.int32),
            V((2, 4, 128, 128), F32),
            V(TABLE.shape, F32),
            V((8, 4, 128, 128), F32),
            V((2, 4, 128, 128), F32),
            V((2, 8, 128, 128), F32),
            V((2, 128, 128), F32),
            V((2, 4, 128, 128), F32),
            V((3, 8, 256, 256), BF16),
            V((2, 2, 8, 256, 256), BF16),
            V((2, 2, 8, 128, 256), BF16),
            V((2, 256, 128), F32),
            V((2, 256, 128), F32),
            V((256, 128), F32),
            V((256, 128), F32),
            V((2, 64, 128), F32),
            V((2, 64, 128), F32),
            V((2, 2, 32, 128), F32),
            V((2, 2, 32, 128), F32),
            V((2, 32, 128), F32),
            V((2, 32, 128), F32),
            V((2, 96, 128), F32),
            V((2, 2, 32, 128), F32),
            pltpu.SemaphoreType.DMA((8,)),
            pltpu.SemaphoreType.DMA((22,)),
            pltpu.SemaphoreType.DMA((22,)),
            pltpu.SemaphoreType.REGULAR((3,)),
        ] + [V(shape, BF16) for shape in SPLITS.values()],
        compiler_params=pltpu.CompilerParams(vmem_limit_bytes=60 * 2**20, collective_id=0, has_side_effects=True),
        name="litho",
    )(mask_field, target, kernel_real, kernel_imag, jnp.asarray(TABLE))
    return pl.pallas_call(
        add_up,
        out_shape=(tile, tile),
        in_specs=[pl.BlockSpec(memory_space=HBM)] * 6,
        out_specs=[pl.BlockSpec(memory_space=HBM)] * 2,
        scratch_shapes=[V(tile.shape, F32)] * 2 + [V(x.shape, F32) for x in landing] + [pltpu.SemaphoreType.DMA((8,))],
        name="add_up",
    )(*results)


def solution(mesh):
    in_specs = (P("row", "col"), P("row", "col"), P(), P())
    out_specs = (P("row", "col"), P("row", "col"))
    return jax.shard_map(local, mesh=mesh, in_specs=in_specs, out_specs=out_specs, check_vma=False)
```

```python
import jax
import jax.numpy as jnp
import numpy as np
from jax import lax
from jax.experimental import pallas as pl
from jax.experimental.pallas import tpu as pltpu
from jax.sharding import PartitionSpec as P

F32, BF16 = jnp.float32, jnp.bfloat16
MESH = pl.DeviceIdType.MESH
steepness = 1.5
threshold = 2.7


def table():
    freq = 2 * np.pi * (np.arange(128) + 0.5) / 256
    col = np.arange(256)
    col = np.where(col < 192, col, col - 256)
    tap = np.arange(128) - 64
    row = np.arange(256)
    both = lambda position, axis: np.concatenate(
        [f(np.outer(position, freq) if axis else np.outer(freq, position)) for f in (np.cos, np.sin)], axis
    )
    back = both(col, 0) * np.repeat([1.0, -1.0], 128)[:, None] / 32768.0
    return np.concatenate([both(tap, 1), both(row, 0), both(col, 1), both(row, 1), back], 0).astype(np.float32)


TABLE = table()
FIRST = 384


def dot(a, b):
    return jnp.dot(a, b, preferred_element_type=F32)


def split(x):
    high = x.astype(BF16)
    return high, (x - high.astype(F32)).astype(BF16)


def lanes(a, b):
    return jnp.concatenate([a, b], axis=1)


def rows(a, b):
    return jnp.concatenate([a, b], axis=0)


def swap(x):
    return pltpu.roll(x, 64, 1)


def butterfly(o):
    cc, cs, sc, ss = o[:128, :128], o[:128, 128:], o[128:, :128], o[128:, 128:]
    return cc - ss, cs + sc, cc + ss, cs - sc


def split_first(tab, t):
    t["wk_hh"][:128], t["wk_l"][...] = split(tab[:128])
    t["wk_hh"][128:] = t["wk_hh"][:128]
    t["cs_h"][...], t["cs_l"][...] = split(tab[128:384])
    t["ca_hh"][:, :128] = t["cs_h"][:, :128]
    t["ca_hh"][:, 128:] = t["cs_h"][:, :128]


def split_second(tab, t):
    t["wm_h"][...], t["wm_l"][...] = split(tab[384:640])
    t["wy_hh"][:128] = t["wm_h"][:128]
    t["wy_hh"][128:] = t["wm_h"][:128]
    t["l2_h"][...], t["l2_l"][...] = split(tab[640:896])
    t["wi_h"][...], t["wi_l"][...] = split(tab[896:1152])
    t["wiy_hl"][:, :128] = t["wi_h"][:, :128]
    t["wiy_hl"][:, 128:] = t["wi_l"][:, :128]


def kernel_spectra(t, k_ref, c_s, H):
    for part in range(2):
        for k in range(4):
            xh, xl = split(k_ref[part, k])
            c = dot(lanes(xh, xl), t["wk_hh"][...]) + dot(xh, t["wk_l"][...])
            c_s[2 * k + part, :128], c_s[2 * k + part, 128:] = split(c)
    for j in range(8):
        o = dot(t["ca_hh"][...], c_s[j]) + dot(t["cs_l"][:, :128], c_s[j, :128])
        for n, v in enumerate(butterfly(o)):
            H[j, n] = v


def mask_spectrum(t, block, M):
    xh, xl = split(block)
    c = dot(xh, t["wm_h"][...]) + dot(xl, t["wm_h"][...]) + dot(xh, t["wm_l"][...])
    ch, cl = split(c)
    o = dot(t["cs_h"][...], ch) + dot(t["cs_h"][...], cl) + dot(t["cs_l"][...], ch)
    for n, v in enumerate(butterfly(o)):
        M[n] = v


def field_rows(t, H, M, d_s, z_s, j):
    def one(n):
        mr, mi, hr, hi = M[n], M[n + 1], H[j, n], H[j, n + 1]
        return mr * hr + mi * hi, mr * hi - mi * hr

    pr, pi = one(0)
    nr, ni = one(2)
    d_s[0, j], d_s[1, j] = split(rows(lanes(pr + nr, pi + ni), lanes(ni - pi, pr - nr)))
    dh, dl = d_s[0, j], d_s[1, j]
    z = dot(t["l2_h"][:128], dh) + dot(t["l2_h"][:128], dl) + dot(t["l2_l"][:128], dh)
    z_s[0, j], z_s[1, j] = split(z)


def field_columns(t, z_s, f, j):
    a = dot(z_s[0, j], t["wiy_hl"][...])
    f[j] = a[:, :128] + a[:, 128:] + dot(z_s[1, j], t["wi_h"][:, :128])


def image(f, target):
    a = f[0] * f[0]
    for j in range(1, 8):
        a = a + f[j] * f[j]
    resist = jax.nn.sigmoid(steepness * (a - threshold))
    return a, 2.0 * (resist - target.astype(F32)) * steepness * resist * (1.0 - resist)


def back_columns(t, f, slope, c_s, j):
    gh, gl = split(slope[...] * f[j])
    c = dot(lanes(gh, gl), t["wy_hh"][...]) + dot(gh, t["wm_l"][:128])
    c_s[j, :128], c_s[j, 128:] = split(c)


def back_rows(t, H, c_s, T, j):
    o = dot(t["ca_hh"][...], c_s[j]) + dot(t["cs_l"][:, :128], c_s[j, :128])
    b = butterfly(o)
    for n in (0, 2):
        gr, gi, hr, hi = b[n], b[n + 1], H[j, n], H[j, n + 1]
        tr, ti = gr * hr - gi * hi, gr * hi + gi * hr
        if j:
            tr, ti = tr + T[n], ti + T[n + 1]
        T[n], T[n + 1] = tr, ti


def final_rows(t, T):
    rp, ip, rm, im = T[0], T[1], T[2], T[3]
    dh, dl = split(2.0 * rows(lanes(rp + rm, -(ip + im)), lanes(ip - im, rp - rm)))
    return split(dot(t["l2_h"][...], dh) + dot(t["l2_h"][...], dl) + dot(t["l2_l"][...], dh))


def final_columns(t, z, which):
    zh, zl = z
    wh, wl = t["wi_h"][:, which], t["wi_l"][:, which]
    return dot(zh, wh) + dot(zl, wh) + dot(zh, wl)


OWN, SIDE = slice(0, 128), slice(128, 256)
SPLITS = dict(
    wk_hh=(256, 256), wk_l=(128, 256), cs_h=(256, 256), cs_l=(256, 256), ca_hh=(256, 256), wm_h=(256, 256),
    wm_l=(256, 256), wy_hh=(256, 256), l2_h=(256, 256), l2_l=(256, 256), wi_h=(256, 256), wi_l=(256, 256),
    wiy_hl=(256, 256),
)


def lower_first(r):
    z = lax.rem(r, 8)
    return jnp.logical_or(z == 0, z == 7)


def kernel(mask, target, kr, ki, tab, aerial, partial, g0_in, g1_in, gc_in, gr_in,
           E, target_v, k_v, tab_v, H, M, f, slope, T, c_s, d_s, z_s, C, S, aerial_v, grad_v,
           side_out, side_in, edge_in, corner_out, corner_in,
           g0_out, g1_out, gc_out, local_sem, send_sem, recv_sem, ready, *splits):
    t = dict(zip(SPLITS, splits))
    r, c = lax.axis_index("row"), lax.axis_index("col")
    nr, nc = lax.axis_size("row"), lax.axis_size("col")
    near = {"u": r > 0, "d": r < nr - 1, "l": c > 0, "r": c < nc - 1}
    shift = {"u": (-1, 0), "d": (1, 0), "l": (0, -1), "r": (0, 1)}
    opposite = {"u": "d", "d": "u", "l": "r", "r": "l"}

    def there(way):
        cond = near[way[0]]
        for w in way[1:]:
            cond = jnp.logical_and(cond, near[w])
        return cond

    def device(way):
        return (r + sum(shift[w][0] for w in way), c + sum(shift[w][1] for w in way))

    local = []
    for n, (src, dst) in enumerate(((mask, E.at[0, pl.ds(64, 256)]), (kr, k_v.at[0]), (ki, k_v.at[1]),
                                    (tab.at[pl.ds(0, FIRST)], tab_v.at[pl.ds(0, FIRST)]),
                                    (tab.at[pl.ds(FIRST, 768)], tab_v.at[pl.ds(FIRST, 768)]), (target, target_v))):
        local.append(pltpu.make_async_copy(src, dst, local_sem.at[n]))
        local[-1].start()

    z = lax.rem(r, 8)
    opens, closes = z == 0, z == 7
    both_hold = jnp.logical_and
    inner_up, inner_down = both_hold(near["u"], jnp.logical_not(opens)), both_hold(near["d"], jnp.logical_not(closes))
    outer_up, outer_down = both_hold(near["u"], opens), both_hold(near["d"], closes)
    odd = lax.rem(lax.div(c, 2), 2) == 1
    across = {"l": both_hold(closes, lax.rem(c, 2) == 0), "r": both_hold(closes, lax.rem(c, 2) == 1)}
    late_here = {way: both_hold(both_hold(near[way], across[way]), odd) for way in "lr"}
    late_there = {way: both_hold(both_hold(near[way], across[way]), jnp.logical_not(odd)) for way in "lr"}
    tells = {"l": both_hold(near["l"], jnp.logical_not(late_here["l"])),
             "r": both_hold(near["r"], jnp.logical_not(late_here["r"])), "u": near["u"], "d": inner_down,
             "ul": both_hold(opens, there("ul")), "ur": both_hold(opens, there("ur"))}
    hears = {"l": both_hold(near["l"], jnp.logical_not(late_there["l"])),
             "r": both_hold(near["r"], jnp.logical_not(late_there["r"])), "u": inner_up, "d": near["d"],
             "dl": both_hold(closes, there("dl")), "dr": both_hold(closes, there("dr"))}
    barrier = pltpu.get_barrier_semaphore()
    for way, cond in tells.items():
        @pl.when(cond)
        def _():
            pl.semaphore_signal(barrier, inc=1, device_id=device(way), device_id_type=MESH)

    def word(sem, way, cond):
        @pl.when(cond)
        def _():
            pl.semaphore_signal(sem, inc=1, device_id=device(way), device_id_type=MESH)

    def hear(sem, cond):
        @pl.when(cond)
        def _():
            pl.semaphore_wait(sem, 1)

    def empty(way, *refs):
        @pl.when(jnp.logical_not(there(way)))
        def _():
            for ref in refs:
                ref[...] = jnp.zeros(ref.shape, F32)

    place = {"l": 0, "r": 1}
    for way in "lr":
        n = 1 - place[way]
        empty(way, side_in.at[n], edge_in.at[:, n])
        empty("u" + way, corner_in.at[n])
    empty("u", E.at[:, pl.ds(0, 64)])
    empty("d", E.at[:, pl.ds(320, 64)])

    lower = lower_first(r)
    upper = jnp.logical_not(lower)
    first = lower.astype(jnp.int32)
    second = 1 - first

    sent = []

    def message(way, src, dst, if_sent=None, if_taken=None):
        n = len(sent)
        copy = pltpu.make_async_remote_copy(src_ref=src, dst_ref=dst, send_sem=send_sem.at[n], recv_sem=recv_sem.at[n],
                                            device_id=device(way), device_id_type=MESH)
        go, come = there(way), there("".join(opposite[w] for w in way))
        go = go if if_sent is None else both_hold(go, if_sent)
        come = come if if_taken is None else both_hold(come, if_taken)
        sent.append((copy, go, come))
        return sent[-1]

    def start(messages, now=None):
        for copy, go, _ in messages:
            @pl.when(go if now is None else both_hold(go, now))
            def _(copy=copy):
                copy.start()

    def arrive(messages, now=None):
        for copy, _, come in messages:
            @pl.when(come if now is None else both_hold(come, now))
            def _(copy=copy):
                copy.wait_recv()

    def is_low(n):
        return lax.broadcasted_iota(jnp.int32, (n, 128), 1) < 64

    def pack(ref, first, second, low_place=0):
        low, second = is_low(first.shape[0]), swap(second)
        ref[low_place] = jnp.where(low, first, second)
        ref[1 - low_place] = jnp.where(low, second, first)

    def both(src, dst, toward="", **when):
        return [message(toward + way, src.at[place[way]], dst.at[place[way]], **when) for way in "lr"]

    side = both(side_out, side_in)
    edges = [both(corner_out.at[1 - k], edge_in.at[k]) for k in range(2)]
    corners = both(corner_out.at[0], corner_in, "d", if_sent=closes, if_taken=opens)
    rows_down = [message("d", E.at[0, pl.ds(256, 64)], E.at[0, pl.ds(0, 64)])]
    rows_up = [message("u", E.at[0, pl.ds(64, 64)], E.at[0, pl.ds(320, 64)])]
    relay_down = [message("d", E.at[1, pl.ds(256, 64)], E.at[1, pl.ds(0, 64)], jnp.logical_not(closes), jnp.logical_not(opens))]
    relay_up = [message("u", E.at[1, pl.ds(64, 64)], E.at[1, pl.ds(320, 64)])]
    from_above = rows_down + relay_down + corners
    from_below = rows_up + relay_up
    corner_above, row_above = both(gc_out.at[0], gc_in.at[1], "u"), [message("u", C.at[first, pl.ds(0, 64)], gr_in.at[1])]
    corner_below, row_below = both(gc_out.at[1], gc_in.at[0], "d"), [message("d", C.at[second, pl.ds(192, 64)], gr_in.at[0])]
    out_edge = both(g0_out, g0_in)
    out_rest = both(g1_out, g1_in)

    local[0].wait()
    pack(side_out, E[0, 128:192], E[0, 192:256])
    pack(corner_out.at[0], E[0, 256:288], E[0, 288:320])
    pack(corner_out.at[1], E[0, 64:96], E[0, 96:128])
    pl.semaphore_wait(barrier, sum(cond.astype(jnp.int32) for cond in hears.values()))
    word(ready.at[0], "d", outer_down)
    for way in "lr":
        word(ready.at[1 + place[way]], way, late_here[way])
    start(corners + rows_down)
    start(rows_up, jnp.logical_not(opens))
    for group in (edges[0], edges[1], side):
        for way in "lr":
            start([group[place[way]]], jnp.logical_not(late_there[way]))

    local[3].wait()
    split_first(tab_v, t)
    local[1].wait()
    local[2].wait()
    kernel_spectra(t, k_v, c_s.at[0], H)
    local[4].wait()
    split_second(tab_v, t)
    local[5].wait()

    def unpack(ref, begin):
        n = ref.shape[1]
        low, from_right, from_left = is_low(n), ref[0], ref[1]
        E[1, pl.ds(begin, n)] = jnp.where(low, from_right, from_left)
        E[1, pl.ds(begin + n, n)] = swap(jnp.where(low, from_left, from_right))

    def spectrum(n, b):
        span = pl.ds(pl.multiple_of(128 * b, 128), 256)
        mask_spectrum(t, lanes(E[0, span], E[1, span]), M.at[n])

    def expose(n, b):
        span = pl.ds(pl.multiple_of(128 * b, 128), 128)
        aerial_v[span], slope[n] = image(f.at[n], target_v[span])

    def outer(b):
        return pl.multiple_of(192 * b, 64)

    def edge(b):
        return pl.multiple_of(64 + 64 * b, 64)

    def pack_outer(n, b):
        start_row = outer(b)
        pack(gc_out.at[b], S[n, pl.ds(start_row, 32)], S[n, pl.ds(start_row + 32, 32)], 1)

    for way in "lr":
        n = place[way]
        hear(ready.at[2 - n], late_there[way])
        start([edges[1][n], edges[0][n], side[n]], late_there[way])
    arrive(edges[0] + edges[1])
    unpack(edge_in.at[0], 64)
    unpack(edge_in.at[1], 256)
    start(relay_down)
    start(relay_up, jnp.logical_not(opens))
    hear(ready.at[0], outer_up)
    start(rows_up + relay_up, opens)
    arrive(side)
    unpack(side_in, 128)
    arrive(from_above, upper)
    arrive(from_below, lower)
    spectrum(0, first)
    for j in range(8):
        field_rows(t, H, M.at[0], d_s.at[0], z_s.at[0], j)
    for j in range(8):
        field_columns(t, z_s.at[0], f.at[0], j)
    expose(0, first)
    for j in range(8):
        back_columns(t, f.at[0], slope.at[0], c_s.at[1], j)
    for j in range(8):
        back_rows(t, H, c_s.at[1], T.at[0], j)
    zz = final_rows(t, T.at[0])
    S[0] = final_columns(t, zz, SIDE)
    pack_outer(0, first)
    edge_row = edge(first)
    pack(g0_out, S[0, pl.ds(edge_row, 32)], S[0, pl.ds(edge_row + 32, 32)], 1)
    start(corner_above, upper)
    start(corner_below, lower)
    start(out_edge)
    C[0] = final_columns(t, zz, OWN)
    start(row_above, upper)
    start(row_below, lower)
    arrive(from_above, lower)
    arrive(from_below, upper)

    @pl.when(opens)
    def _():
        unpack(corner_in, 0)

    spectrum(1, second)
    for j in range(8):
        field_rows(t, H, M.at[1], d_s.at[1], z_s.at[1], j)
    for j in range(8):
        field_columns(t, z_s.at[1], f.at[1], j)
    expose(1, second)
    aerial_out = pltpu.make_async_copy(aerial_v, aerial, local_sem.at[6])
    aerial_out.start()
    for j in range(8):
        back_columns(t, f.at[1], slope.at[1], c_s.at[2], j)
    for j in range(8):
        back_rows(t, H, c_s.at[2], T.at[1], j)
    zz = final_rows(t, T.at[1])
    S[1] = final_columns(t, zz, SIDE)
    pack_outer(1, second)
    middle = S[first, 128:256] + S[second, 0:128]
    pack(g1_out, middle[:96], rows(middle[96:], S[1, pl.ds(edge(second), 64)]), 1)
    start(out_rest)
    start(corner_above, lower)
    start(corner_below, upper)
    C[1] = final_columns(t, zz, OWN)
    start(row_above, lower)
    start(row_below, upper)
    grad_v[:64] = C[first, 64:128]
    grad_v[64:192] = C[first, 128:256] + C[second, 0:128]
    grad_v[192:] = C[second, 128:192]

    partial_out = pltpu.make_async_copy(grad_v, partial, local_sem.at[7])
    partial_out.start()
    arrive(out_edge + out_rest + corner_above + corner_below + row_above + row_below)
    for copy, go, _ in sent:
        @pl.when(go)
        def _():
            copy.wait_send()
    aerial_out.wait()
    partial_out.wait()


def add_up(aerial, partial, g0, g1, gc, gr, aerial_out, gradient_out,
           aerial_v, grad_v, g0_v, g1_v, gc_v, gr_v, sem):
    ins = [pltpu.make_async_copy(src, dst, sem.at[n]) for n, (src, dst) in enumerate((
        (aerial, aerial_v), (partial, grad_v), (g0, g0_v), (g1, g1_v), (gc, gc_v), (gr, gr_v)))]
    for copy in ins:
        copy.start()
    r, c = lax.axis_index("row"), lax.axis_index("col")
    nr, nc = lax.axis_size("row"), lax.axis_size("col")
    up, down, left, right = r > 0, r < nr - 1, c > 0, c < nc - 1
    first = lower_first(r).astype(jnp.int32)

    def gain(ref, cond=None):
        from_right, from_left = ref[0], ref[1]
        here_right = right if cond is None else jnp.logical_and(right, cond)
        here_left = left if cond is None else jnp.logical_and(left, cond)
        from_right = jnp.where(here_right, from_right, 0.0)
        from_left = jnp.where(here_left, from_left, 0.0)
        low = lax.broadcasted_iota(jnp.int32, from_left.shape, 1) < 64
        return rows(jnp.where(low, from_left, from_right), swap(jnp.where(low, from_right, from_left)))

    ins[0].wait()
    aerial_copy = pltpu.make_async_copy(aerial_v, aerial_out, sem.at[6])
    aerial_copy.start()
    for copy in ins[1:]:
        copy.wait()
    rest = gain(g1_v)
    grad_v[64:192] += rest[:128]
    grad_v[pl.ds(pl.multiple_of(192 * (1 - first), 64), 64)] += rest[128:]
    grad_v[pl.ds(pl.multiple_of(192 * first, 64), 64)] += gain(g0_v)
    grad_v[:64] += gain(gc_v.at[0], up) + jnp.where(up, gr_v[0], 0.0)
    grad_v[192:] += gain(gc_v.at[1], down) + jnp.where(down, gr_v[1], 0.0)
    gradient_copy = pltpu.make_async_copy(grad_v, gradient_out, sem.at[7])
    gradient_copy.start()
    aerial_copy.wait()
    gradient_copy.wait()


def local(mask_field, target, kernel_real, kernel_imag):
    V, HBM = pltpu.VMEM, pltpu.HBM
    tile = jax.ShapeDtypeStruct(mask_field.shape, F32)
    landing = tuple(jax.ShapeDtypeStruct(shape, F32) for shape in ((2, 32, 128), (2, 96, 128), (2, 2, 32, 128), (2, 64, 128)))
    results = pl.pallas_call(
        kernel,
        out_shape=(tile, tile) + landing,
        in_specs=[pl.BlockSpec(memory_space=HBM)] * 5,
        out_specs=[pl.BlockSpec(memory_space=HBM)] * 6,
        scratch_shapes=[
            V((2, 384, 128), F32),
            V((256, 128), jnp.int32),
            V((2, 4, 128, 128), F32),
            V(TABLE.shape, F32),
            V((8, 4, 128, 128), F32),
            V((2, 4, 128, 128), F32),
            V((2, 8, 128, 128), F32),
            V((2, 128, 128), F32),
            V((2, 4, 128, 128), F32),
            V((3, 8, 256, 256), BF16),
            V((2, 2, 8, 256, 256), BF16),
            V((2, 2, 8, 128, 256), BF16),
            V((2, 256, 128), F32),
            V((2, 256, 128), F32),
            V((256, 128), F32),
            V((256, 128), F32),
            V((2, 64, 128), F32),
            V((2, 64, 128), F32),
            V((2, 2, 32, 128), F32),
            V((2, 2, 32, 128), F32),
            V((2, 32, 128), F32),
            V((2, 32, 128), F32),
            V((2, 96, 128), F32),
            V((2, 2, 32, 128), F32),
            pltpu.SemaphoreType.DMA((8,)),
            pltpu.SemaphoreType.DMA((22,)),
            pltpu.SemaphoreType.DMA((22,)),
            pltpu.SemaphoreType.REGULAR((3,)),
        ] + [V(shape, BF16) for shape in SPLITS.values()],
        compiler_params=pltpu.CompilerParams(vmem_limit_bytes=60 * 2**20, collective_id=0, has_side_effects=True),
        name="litho",
    )(mask_field, target, kernel_real, kernel_imag, jnp.asarray(TABLE))
    return pl.pallas_call(
        add_up,
        out_shape=(tile, tile),
        in_specs=[pl.BlockSpec(memory_space=HBM)] * 6,
        out_specs=[pl.BlockSpec(memory_space=HBM)] * 2,
        scratch_shapes=[V(tile.shape, F32)] * 2 + [V(x.shape, F32) for x in landing] + [pltpu.SemaphoreType.DMA((8,))],
        name="add_up",
    )(*results)


def solution(mesh):
    in_specs = (P("row", "col"), P("row", "col"), P(), P())
    out_specs = (P("row", "col"), P("row", "col"))
    return jax.shard_map(local, mesh=mesh, in_specs=in_specs, out_specs=out_specs, check_vma=False)
```

```python
import jax
import jax.numpy as jnp
import numpy as np
from jax import lax
from jax.experimental import pallas as pl
from jax.experimental.pallas import tpu as pltpu
from jax.sharding import PartitionSpec as P

F32, BF16 = jnp.float32, jnp.bfloat16
MESH = pl.DeviceIdType.MESH
steepness = 1.5
threshold = 2.7


def table():
    freq = 2 * np.pi * (np.arange(128) + 0.5) / 256
    col = np.arange(256)
    col = np.where(col < 192, col, col - 256)
    tap = np.arange(128) - 64
    row = np.arange(256)
    both = lambda position, axis: np.concatenate(
        [f(np.outer(position, freq) if axis else np.outer(freq, position)) for f in (np.cos, np.sin)], axis
    )
    back = both(col, 0) * np.repeat([1.0, -1.0], 128)[:, None] / 32768.0
    return np.concatenate([both(tap, 1), both(row, 0), both(col, 1), both(row, 1), back], 0).astype(np.float32)


TABLE = table()
FIRST = 384


def dot(a, b):
    return jnp.dot(a, b, preferred_element_type=F32)


def split(x):
    high = x.astype(BF16)
    return high, (x - high.astype(F32)).astype(BF16)


def lanes(a, b):
    return jnp.concatenate([a, b], axis=1)


def rows(a, b):
    return jnp.concatenate([a, b], axis=0)


def swap(x):
    return pltpu.roll(x, 64, 1)


def butterfly(o):
    cc, cs, sc, ss = o[:128, :128], o[:128, 128:], o[128:, :128], o[128:, 128:]
    return cc - ss, cs + sc, cc + ss, cs - sc


def split_first(tab, t):
    t["wk_hh"][:128], t["wk_l"][...] = split(tab[:128])
    t["wk_hh"][128:] = t["wk_hh"][:128]
    t["cs_h"][...], t["cs_l"][...] = split(tab[128:384])
    t["ca_hh"][:, :128] = t["cs_h"][:, :128]
    t["ca_hh"][:, 128:] = t["cs_h"][:, :128]


def split_second(tab, t):
    t["wm_h"][...], t["wm_l"][...] = split(tab[384:640])
    t["wy_hh"][:128] = t["wm_h"][:128]
    t["wy_hh"][128:] = t["wm_h"][:128]
    t["l2_h"][...], t["l2_l"][...] = split(tab[640:896])
    t["wi_h"][...], t["wi_l"][...] = split(tab[896:1152])
    t["wiy_hl"][:, :128] = t["wi_h"][:, :128]
    t["wiy_hl"][:, 128:] = t["wi_l"][:, :128]


def kernel_spectra(t, k_ref, c_s, H):
    for part in range(2):
        for k in range(4):
            xh, xl = split(k_ref[part, k])
            c = dot(lanes(xh, xl), t["wk_hh"][...]) + dot(xh, t["wk_l"][...])
            c_s[2 * k + part, :128], c_s[2 * k + part, 128:] = split(c)
    for j in range(8):
        o = dot(t["ca_hh"][...], c_s[j]) + dot(t["cs_l"][:, :128], c_s[j, :128])
        for n, v in enumerate(butterfly(o)):
            H[j, n] = v


def mask_spectrum(t, block, M):
    xh, xl = split(block)
    c = dot(xh, t["wm_h"][...]) + dot(xl, t["wm_h"][...]) + dot(xh, t["wm_l"][...])
    ch, cl = split(c)
    o = dot(t["cs_h"][...], ch) + dot(t["cs_h"][...], cl) + dot(t["cs_l"][...], ch)
    for n, v in enumerate(butterfly(o)):
        M[n] = v


def field_rows(t, H, M, d_s, z_s, j):
    def one(n):
        mr, mi, hr, hi = M[n], M[n + 1], H[j, n], H[j, n + 1]
        return mr * hr + mi * hi, mr * hi - mi * hr

    pr, pi = one(0)
    nr, ni = one(2)
    d_s[0, j], d_s[1, j] = split(rows(lanes(pr + nr, pi + ni), lanes(ni - pi, pr - nr)))
    dh, dl = d_s[0, j], d_s[1, j]
    z = dot(t["l2_h"][:128], dh) + dot(t["l2_h"][:128], dl) + dot(t["l2_l"][:128], dh)
    z_s[0, j], z_s[1, j] = split(z)


def field_columns(t, z_s, f, j):
    a = dot(z_s[0, j], t["wiy_hl"][...])
    f[j] = a[:, :128] + a[:, 128:] + dot(z_s[1, j], t["wi_h"][:, :128])


def image(f, target):
    a = f[0] * f[0]
    for j in range(1, 8):
        a = a + f[j] * f[j]
    resist = jax.nn.sigmoid(steepness * (a - threshold))
    return a, 2.0 * (resist - target.astype(F32)) * steepness * resist * (1.0 - resist)


def back_columns(t, f, slope, c_s, j):
    gh, gl = split(slope[...] * f[j])
    c = dot(lanes(gh, gl), t["wy_hh"][...]) + dot(gh, t["wm_l"][:128])
    c_s[j, :128], c_s[j, 128:] = split(c)


def back_rows(t, H, c_s, T, j):
    o = dot(t["ca_hh"][...], c_s[j]) + dot(t["cs_l"][:, :128], c_s[j, :128])
    b = butterfly(o)
    for n in (0, 2):
        gr, gi, hr, hi = b[n], b[n + 1], H[j, n], H[j, n + 1]
        tr, ti = gr * hr - gi * hi, gr * hi + gi * hr
        if j:
            tr, ti = tr + T[n], ti + T[n + 1]
        T[n], T[n + 1] = tr, ti


def final_rows(t, T):
    rp, ip, rm, im = T[0], T[1], T[2], T[3]
    dh, dl = split(2.0 * rows(lanes(rp + rm, -(ip + im)), lanes(ip - im, rp - rm)))
    return split(dot(t["l2_h"][...], dh) + dot(t["l2_h"][...], dl) + dot(t["l2_l"][...], dh))


def final_columns(t, z, which):
    zh, zl = z
    wh, wl = t["wi_h"][:, which], t["wi_l"][:, which]
    return dot(zh, wh) + dot(zl, wh) + dot(zh, wl)


OWN, SIDE = slice(0, 128), slice(128, 256)
SPLITS = dict(
    wk_hh=(256, 256), wk_l=(128, 256), cs_h=(256, 256), cs_l=(256, 256), ca_hh=(256, 256), wm_h=(256, 256),
    wm_l=(256, 256), wy_hh=(256, 256), l2_h=(256, 256), l2_l=(256, 256), wi_h=(256, 256), wi_l=(256, 256),
    wiy_hl=(256, 256),
)


def lower_first(r):
    z = lax.rem(r, 8)
    return jnp.logical_or(z == 0, z == 7)


def kernel(mask, target, kr, ki, tab, aerial, partial, g0_in, g1_in, gc_in, gr_in,
           E, target_v, k_v, tab_v, H, M, f, slope, T, c_s, d_s, z_s, C, S, aerial_v, grad_v,
           side_out, side_in, edge_in, corner_out, corner_in,
           g0_out, g1_out, gc_out, local_sem, send_sem, recv_sem, ready, *splits):
    t = dict(zip(SPLITS, splits))
    r, c = lax.axis_index("row"), lax.axis_index("col")
    nr, nc = lax.axis_size("row"), lax.axis_size("col")
    near = {"u": r > 0, "d": r < nr - 1, "l": c > 0, "r": c < nc - 1}
    shift = {"u": (-1, 0), "d": (1, 0), "l": (0, -1), "r": (0, 1)}
    opposite = {"u": "d", "d": "u", "l": "r", "r": "l"}

    def there(way):
        cond = near[way[0]]
        for w in way[1:]:
            cond = jnp.logical_and(cond, near[w])
        return cond

    def device(way):
        return (r + sum(shift[w][0] for w in way), c + sum(shift[w][1] for w in way))

    z = lax.rem(r, 8)
    opens, closes = z == 0, z == 7
    both_hold = jnp.logical_and
    inner_up, inner_down = both_hold(near["u"], jnp.logical_not(opens)), both_hold(near["d"], jnp.logical_not(closes))
    outer_up, outer_down = both_hold(near["u"], opens), both_hold(near["d"], closes)
    odd = lax.rem(lax.div(c, 2), 2) == 1
    across = {"l": both_hold(closes, lax.rem(c, 2) == 0), "r": both_hold(closes, lax.rem(c, 2) == 1)}
    late_here = {way: both_hold(both_hold(near[way], across[way]), odd) for way in "lr"}
    late_there = {way: both_hold(both_hold(near[way], across[way]), jnp.logical_not(odd)) for way in "lr"}
    tells = {"l": both_hold(near["l"], jnp.logical_not(late_here["l"])),
             "r": both_hold(near["r"], jnp.logical_not(late_here["r"])), "u": near["u"], "d": inner_down,
             "ul": both_hold(opens, there("ul")), "ur": both_hold(opens, there("ur"))}
    hears = {"l": both_hold(near["l"], jnp.logical_not(late_there["l"])),
             "r": both_hold(near["r"], jnp.logical_not(late_there["r"])), "u": inner_up, "d": near["d"],
             "dl": both_hold(closes, there("dl")), "dr": both_hold(closes, there("dr"))}
    barrier = pltpu.get_barrier_semaphore()
    for way, cond in tells.items():
        @pl.when(cond)
        def _():
            pl.semaphore_signal(barrier, inc=1, device_id=device(way), device_id_type=MESH)

    local = []
    for n, (src, dst) in enumerate(((mask, E.at[0, pl.ds(64, 256)]), (kr, k_v.at[0]), (ki, k_v.at[1]),
                                    (tab.at[pl.ds(0, FIRST)], tab_v.at[pl.ds(0, FIRST)]),
                                    (tab.at[pl.ds(FIRST, 768)], tab_v.at[pl.ds(FIRST, 768)]), (target, target_v))):
        local.append(pltpu.make_async_copy(src, dst, local_sem.at[n]))
        local[-1].start()

    def word(sem, way, cond):
        @pl.when(cond)
        def _():
            pl.semaphore_signal(sem, inc=1, device_id=device(way), device_id_type=MESH)

    def hear(sem, cond):
        @pl.when(cond)
        def _():
            pl.semaphore_wait(sem, 1)

    def empty(way, *refs):
        @pl.when(jnp.logical_not(there(way)))
        def _():
            for ref in refs:
                ref[...] = jnp.zeros(ref.shape, F32)

    place = {"l": 0, "r": 1}
    for way in "lr":
        n = 1 - place[way]
        empty(way, side_in.at[n], edge_in.at[:, n])
        empty("u" + way, corner_in.at[n])
    empty("u", E.at[:, pl.ds(0, 64)])
    empty("d", E.at[:, pl.ds(320, 64)])

    lower = lower_first(r)
    upper = jnp.logical_not(lower)
    first = lower.astype(jnp.int32)
    second = 1 - first

    sent = []

    def message(way, src, dst, if_sent=None, if_taken=None):
        n = len(sent)
        copy = pltpu.make_async_remote_copy(src_ref=src, dst_ref=dst, send_sem=send_sem.at[n], recv_sem=recv_sem.at[n],
                                            device_id=device(way), device_id_type=MESH)
        go, come = there(way), there("".join(opposite[w] for w in way))
        go = go if if_sent is None else both_hold(go, if_sent)
        come = come if if_taken is None else both_hold(come, if_taken)
        sent.append((copy, go, come))
        return sent[-1]

    def start(messages, now=None):
        for copy, go, _ in messages:
            @pl.when(go if now is None else both_hold(go, now))
            def _(copy=copy):
                copy.start()

    def arrive(messages, now=None):
        for copy, _, come in messages:
            @pl.when(come if now is None else both_hold(come, now))
            def _(copy=copy):
                copy.wait_recv()

    def is_low(n):
        return lax.broadcasted_iota(jnp.int32, (n, 128), 1) < 64

    def pack(ref, first, second, low_place=0):
        low, second = is_low(first.shape[0]), swap(second)
        ref[low_place] = jnp.where(low, first, second)
        ref[1 - low_place] = jnp.where(low, second, first)

    def both(src, dst, toward="", **when):
        return [message(toward + way, src.at[place[way]], dst.at[place[way]], **when) for way in "lr"]

    side = both(side_out, side_in)
    edges = [both(corner_out.at[1 - k], edge_in.at[k]) for k in range(2)]
    corners = both(corner_out.at[0], corner_in, "d", if_sent=closes, if_taken=opens)
    rows_down = [message("d", E.at[0, pl.ds(256, 64)], E.at[0, pl.ds(0, 64)])]
    rows_up = [message("u", E.at[0, pl.ds(64, 64)], E.at[0, pl.ds(320, 64)])]
    relay_down = [message("d", E.at[1, pl.ds(256, 64)], E.at[1, pl.ds(0, 64)], jnp.logical_not(closes), jnp.logical_not(opens))]
    relay_up = [message("u", E.at[1, pl.ds(64, 64)], E.at[1, pl.ds(320, 64)])]
    from_above = rows_down + relay_down + corners
    from_below = rows_up + relay_up
    corner_above, row_above = both(gc_out.at[0], gc_in.at[1], "u"), [message("u", C.at[first, pl.ds(0, 64)], gr_in.at[1])]
    corner_below, row_below = both(gc_out.at[1], gc_in.at[0], "d"), [message("d", C.at[second, pl.ds(192, 64)], gr_in.at[0])]
    out_edge = both(g0_out, g0_in)
    out_rest = both(g1_out, g1_in)

    local[0].wait()
    pack(side_out, E[0, 128:192], E[0, 192:256])
    pack(corner_out.at[0], E[0, 256:288], E[0, 288:320])
    pack(corner_out.at[1], E[0, 64:96], E[0, 96:128])
    pl.semaphore_wait(barrier, sum(cond.astype(jnp.int32) for cond in hears.values()))
    word(ready.at[0], "d", outer_down)
    for way in "lr":
        word(ready.at[1 + place[way]], way, late_here[way])
    start(corners + rows_down)
    start(rows_up, jnp.logical_not(opens))
    for group in (edges[0], edges[1], side):
        for way in "lr":
            start([group[place[way]]], jnp.logical_not(late_there[way]))

    local[3].wait()
    split_first(tab_v, t)
    local[1].wait()
    local[2].wait()
    kernel_spectra(t, k_v, c_s.at[0], H)
    local[4].wait()
    split_second(tab_v, t)
    local[5].wait()

    def unpack(ref, begin):
        n = ref.shape[1]
        low, from_right, from_left = is_low(n), ref[0], ref[1]
        E[1, pl.ds(begin, n)] = jnp.where(low, from_right, from_left)
        E[1, pl.ds(begin + n, n)] = swap(jnp.where(low, from_left, from_right))

    def spectrum(n, b):
        span = pl.ds(pl.multiple_of(128 * b, 128), 256)
        mask_spectrum(t, lanes(E[0, span], E[1, span]), M.at[n])

    def expose(n, b):
        span = pl.ds(pl.multiple_of(128 * b, 128), 128)
        aerial_v[span], slope[n] = image(f.at[n], target_v[span])

    def outer(b):
        return pl.multiple_of(192 * b, 64)

    def edge(b):
        return pl.multiple_of(64 + 64 * b, 64)

    def pack_outer(n, b):
        start_row = outer(b)
        pack(gc_out.at[b], S[n, pl.ds(start_row, 32)], S[n, pl.ds(start_row + 32, 32)], 1)

    for way in "lr":
        n = place[way]
        hear(ready.at[2 - n], late_there[way])
        start([edges[1][n], edges[0][n], side[n]], late_there[way])
    arrive(edges[0] + edges[1])
    unpack(edge_in.at[0], 64)
    unpack(edge_in.at[1], 256)
    start(relay_down)
    start(relay_up, jnp.logical_not(opens))
    hear(ready.at[0], outer_up)
    start(rows_up + relay_up, opens)
    arrive(side)
    unpack(side_in, 128)
    arrive(from_above, upper)
    arrive(from_below, lower)
    spectrum(0, first)
    for j in range(8):
        field_rows(t, H, M.at[0], d_s.at[0], z_s.at[0], j)
    for j in range(8):
        field_columns(t, z_s.at[0], f.at[0], j)
    expose(0, first)
    for j in range(8):
        back_columns(t, f.at[0], slope.at[0], c_s.at[1], j)
    for j in range(8):
        back_rows(t, H, c_s.at[1], T.at[0], j)
    zz = final_rows(t, T.at[0])
    S[0] = final_columns(t, zz, SIDE)
    pack_outer(0, first)
    edge_row = edge(first)
    pack(g0_out, S[0, pl.ds(edge_row, 32)], S[0, pl.ds(edge_row + 32, 32)], 1)
    start(corner_above, upper)
    start(corner_below, lower)
    start(out_edge)
    C[0] = final_columns(t, zz, OWN)
    start(row_above, upper)
    start(row_below, lower)
    arrive(from_above, lower)
    arrive(from_below, upper)

    @pl.when(opens)
    def _():
        unpack(corner_in, 0)

    spectrum(1, second)
    for j in range(8):
        field_rows(t, H, M.at[1], d_s.at[1], z_s.at[1], j)
    for j in range(8):
        field_columns(t, z_s.at[1], f.at[1], j)
    expose(1, second)
    aerial_out = pltpu.make_async_copy(aerial_v, aerial, local_sem.at[6])
    aerial_out.start()
    for j in range(8):
        back_columns(t, f.at[1], slope.at[1], c_s.at[2], j)
    for j in range(8):
        back_rows(t, H, c_s.at[2], T.at[1], j)
    zz = final_rows(t, T.at[1])
    S[1] = final_columns(t, zz, SIDE)
    pack_outer(1, second)
    middle = S[first, 128:256] + S[second, 0:128]
    pack(g1_out, middle[:96], rows(middle[96:], S[1, pl.ds(edge(second), 64)]), 1)
    start(out_rest)
    start(corner_above, lower)
    start(corner_below, upper)
    C[1] = final_columns(t, zz, OWN)
    start(row_above, lower)
    start(row_below, upper)
    grad_v[:64] = C[first, 64:128]
    grad_v[64:192] = C[first, 128:256] + C[second, 0:128]
    grad_v[192:] = C[second, 128:192]

    partial_out = pltpu.make_async_copy(grad_v, partial, local_sem.at[7])
    partial_out.start()
    arrive(out_edge + out_rest + corner_above + corner_below + row_above + row_below)
    for copy, go, _ in sent:
        @pl.when(go)
        def _():
            copy.wait_send()
    aerial_out.wait()
    partial_out.wait()


def add_up(aerial, partial, g0, g1, gc, gr, aerial_out, gradient_out,
           aerial_v, grad_v, g0_v, g1_v, gc_v, gr_v, sem):
    ins = [pltpu.make_async_copy(src, dst, sem.at[n]) for n, (src, dst) in enumerate((
        (aerial, aerial_v), (partial, grad_v), (g0, g0_v), (g1, g1_v), (gc, gc_v), (gr, gr_v)))]
    for copy in ins:
        copy.start()
    r, c = lax.axis_index("row"), lax.axis_index("col")
    nr, nc = lax.axis_size("row"), lax.axis_size("col")
    up, down, left, right = r > 0, r < nr - 1, c > 0, c < nc - 1
    first = lower_first(r).astype(jnp.int32)

    def gain(ref, cond=None):
        from_right, from_left = ref[0], ref[1]
        here_right = right if cond is None else jnp.logical_and(right, cond)
        here_left = left if cond is None else jnp.logical_and(left, cond)
        from_right = jnp.where(here_right, from_right, 0.0)
        from_left = jnp.where(here_left, from_left, 0.0)
        low = lax.broadcasted_iota(jnp.int32, from_left.shape, 1) < 64
        return rows(jnp.where(low, from_left, from_right), swap(jnp.where(low, from_right, from_left)))

    ins[0].wait()
    aerial_copy = pltpu.make_async_copy(aerial_v, aerial_out, sem.at[6])
    aerial_copy.start()
    for copy in ins[1:]:
        copy.wait()
    rest = gain(g1_v)
    grad_v[64:192] += rest[:128]
    grad_v[pl.ds(pl.multiple_of(192 * (1 - first), 64), 64)] += rest[128:]
    grad_v[pl.ds(pl.multiple_of(192 * first, 64), 64)] += gain(g0_v)
    grad_v[:64] += gain(gc_v.at[0], up) + jnp.where(up, gr_v[0], 0.0)
    grad_v[192:] += gain(gc_v.at[1], down) + jnp.where(down, gr_v[1], 0.0)
    gradient_copy = pltpu.make_async_copy(grad_v, gradient_out, sem.at[7])
    gradient_copy.start()
    aerial_copy.wait()
    gradient_copy.wait()


def local(mask_field, target, kernel_real, kernel_imag):
    V, HBM = pltpu.VMEM, pltpu.HBM
    tile = jax.ShapeDtypeStruct(mask_field.shape, F32)
    landing = tuple(jax.ShapeDtypeStruct(shape, F32) for shape in ((2, 32, 128), (2, 96, 128), (2, 2, 32, 128), (2, 64, 128)))
    results = pl.pallas_call(
        kernel,
        out_shape=(tile, tile) + landing,
        in_specs=[pl.BlockSpec(memory_space=HBM)] * 5,
        out_specs=[pl.BlockSpec(memory_space=HBM)] * 6,
        scratch_shapes=[
            V((2, 384, 128), F32),
            V((256, 128), jnp.int32),
            V((2, 4, 128, 128), F32),
            V(TABLE.shape, F32),
            V((8, 4, 128, 128), F32),
            V((2, 4, 128, 128), F32),
            V((2, 8, 128, 128), F32),
            V((2, 128, 128), F32),
            V((2, 4, 128, 128), F32),
            V((3, 8, 256, 256), BF16),
            V((2, 2, 8, 256, 256), BF16),
            V((2, 2, 8, 128, 256), BF16),
            V((2, 256, 128), F32),
            V((2, 256, 128), F32),
            V((256, 128), F32),
            V((256, 128), F32),
            V((2, 64, 128), F32),
            V((2, 64, 128), F32),
            V((2, 2, 32, 128), F32),
            V((2, 2, 32, 128), F32),
            V((2, 32, 128), F32),
            V((2, 32, 128), F32),
            V((2, 96, 128), F32),
            V((2, 2, 32, 128), F32),
            pltpu.SemaphoreType.DMA((8,)),
            pltpu.SemaphoreType.DMA((22,)),
            pltpu.SemaphoreType.DMA((22,)),
            pltpu.SemaphoreType.REGULAR((3,)),
        ] + [V(shape, BF16) for shape in SPLITS.values()],
        compiler_params=pltpu.CompilerParams(vmem_limit_bytes=60 * 2**20, collective_id=0, has_side_effects=True),
        name="litho",
    )(mask_field, target, kernel_real, kernel_imag, jnp.asarray(TABLE))
    return pl.pallas_call(
        add_up,
        out_shape=(tile, tile),
        in_specs=[pl.BlockSpec(memory_space=HBM)] * 6,
        out_specs=[pl.BlockSpec(memory_space=HBM)] * 2,
        scratch_shapes=[V(tile.shape, F32)] * 2 + [V(x.shape, F32) for x in landing] + [pltpu.SemaphoreType.DMA((8,))],
        name="add_up",
    )(*results)


def solution(mesh):
    in_specs = (P("row", "col"), P("row", "col"), P(), P())
    out_specs = (P("row", "col"), P("row", "col"))
    return jax.shard_map(local, mesh=mesh, in_specs=in_specs, out_specs=out_specs, check_vma=False)
```
